512 devices in a mesh: comp: 8 (over y, core), tile: 64 (over x, z).
Axes of the slice: x: 4, y: 4, z: 16, core: 2. Of those that a mesh axis runs over, the one named last changes fastest.
Arguments:
- spectrum: float32 [1296, 256, 512], P('comp', 'tile'), may hold values from 0.05 to 1
- sea_mask: int32 [256, 512], P('tile'), may hold values 0 or 1
- quad_bins: int32 [4, 1296], replicated, may hold values from 0 to 1295
- coupling: float32 [1296], replicated, may hold values from 0.05 to 0.5
- growth: float32 [1296], replicated, may hold values from -0.2 to 0.4
Outputs:
- updated: float32 [1296, 256, 512], P('comp', 'tile')
The draws below stay inside these ranges and needn't reach their ends.
All inputs are finite; a program needn't handle non-finite values. No bound on the sum of `sea_mask` on one device may be relied on, other than what follows from the above.
Results may differ from the reference program's by a relative error of at most 0.0001.
Values sent between devices are 32-bit elements; how exact they have to be, the bound alone decides.
No kernel may reach another device: no remote copies, remote signals or barrier semaphores. Data moves between devices by JAX's collectives and lax.ppermute only.
A program may use at most 192 MiB of HBM per device.

```python
import math
import jax
import jax.numpy as jnp
from jax import lax

NDIR = 36
NFREQ = 36
NK = 1296
GY = 512
SUB = 4
NX = 256


def set_ends(values, own_key, low, high):
    longest = values.shape.index(max(values.shape))
    spots = []
    for shift in (0, 1):
        where = [jax.random.randint(jax.random.fold_in(own_key, axis), (), 0, length) for axis, length in enumerate(values.shape)]
        where[longest] = (where[longest] + shift) % values.shape[longest]
        spots.append(tuple(where))
    return values.at[spots[0]].set(low).at[spots[1]].set(high)


def block_levels(stream_key, extent, shards, low, high):
    def one(axis_at, shards_of):
        heights = jax.random.uniform(jax.random.fold_in(jax.random.fold_in(stream_key, 6), axis_at), (shards_of,), jnp.float32, low / len(shards), high / len(shards))
        return jnp.repeat(jnp.exp(heights), extent[axis_at] // shards_of).reshape((-1,) + (1,) * (len(extent) - axis_at - 1))

    loudness = one(*shards[0])
    for cut in shards[1:]:
        loudness = loudness * one(*cut)
    return loudness


def setup_inputs(seed: int = 0) -> dict:
    key_list = jax.random.split(jax.random.key(seed), 6)
    return {
        "spectrum": jnp.clip(jnp.exp(math.log(1.0) - 2.9957323 * jax.random.uniform(key_list[0], (NK, NX, GY), jnp.float32) ** block_levels(key_list[0], (NK, NX, GY), ((0, 8), (1, 64)), -0.2, 0.2)), 0.05, 1.0),
        "sea_mask": set_ends((jax.random.randint(key_list[1], (NX, GY), 0, 4) < 3).astype(jnp.int32), jax.random.fold_in(key_list[1], 1), 0, 1),
        "quad_bins": set_ends(jax.random.randint(key_list[2], (4, NK), 0, NK), jax.random.fold_in(key_list[2], 1), 0, NK - 1).astype(jnp.int32),
        "coupling": jnp.clip(jnp.exp(jax.random.uniform(key_list[3], (NK,), jnp.float32, math.log(0.05), math.log(0.5))), 0.05, 0.5),
        "growth": jnp.clip(jax.random.uniform(key_list[4], (NK,), jnp.float32, -0.2, 0.4), -0.2, 0.4),
    }


w_plus = 0.4096
w_minus = 3.1605
w_cross = 1.2945
time_step = 0.5


def courant_numbers(index):
    direction = (index // NFREQ).astype(jnp.float32)
    level = (index % NFREQ).astype(jnp.float32)
    angle = 2.0 * math.pi * direction / NDIR
    magnitude = 0.7 * jnp.power(jnp.float32(0.93), level)
    return magnitude * jnp.cos(angle), magnitude * jnp.sin(angle)


def advect(extended, along_x, along_y, mask):
    center = extended[:, 1:-1, :]
    west = extended[:, :-2, :]
    east = extended[:, 2:, :]
    padded_y = jnp.pad(center, ((0, 0), (0, 0), (1, 1)))
    south = padded_y[:, :, :-2]
    north = padded_y[:, :, 2:]
    pos_x = jnp.maximum(along_x, 0.0)[:, None, None]
    neg_x = jnp.minimum(along_x, 0.0)[:, None, None]
    pos_y = jnp.maximum(along_y, 0.0)[:, None, None]
    neg_y = jnp.minimum(along_y, 0.0)[:, None, None]
    moved = center - pos_x * (center - west) - neg_x * (east - center)
    moved = moved - pos_y * (center - south) - neg_y * (north - center)
    return moved * mask


def settle(energy, quad_bins, coupling, growth):
    count = energy.shape[0]
    total = growth[:, None] * energy
    for mirror in range(2):
        plus_bins = quad_bins[2 * mirror]
        minus_bins = quad_bins[2 * mirror + 1]
        plus_energy = jnp.take(energy, plus_bins, axis=0)
        minus_energy = jnp.take(energy, minus_bins, axis=0)
        delta = coupling[:, None] * (energy * energy * (w_plus * plus_energy + w_minus * minus_energy)
                                     - 2.0 * w_cross * energy * plus_energy * minus_energy)
        total = total - 2.0 * delta
        total = total + jax.ops.segment_sum(delta, plus_bins, num_segments=count)
        total = total + jax.ops.segment_sum(delta, minus_bins, num_segments=count)
    return energy + time_step * total


def reference(spectrum, sea_mask, quad_bins, coupling, growth):
    along_x, along_y = courant_numbers(jnp.arange(NDIR * NFREQ, dtype=jnp.int32))
    mask = sea_mask.astype(jnp.float32)[None]
    blocks = spectrum.reshape(NDIR, NFREQ, NX, GY)

    def propagate(inputs):
        field, speed_x, speed_y = inputs
        for step in range(SUB):
            extended = jnp.pad(field, ((0, 0), (1, 1), (0, 0)))
            field = advect(extended, speed_x, speed_y, mask)
        return field

    moved = lax.map(propagate, (blocks, along_x.reshape(NDIR, NFREQ), along_y.reshape(NDIR, NFREQ)))
    columns = jnp.moveaxis(moved.reshape(NDIR * NFREQ, NX, GY), 1, 0)
    settled = lax.map(lambda column: settle(column, quad_bins, coupling, growth), columns)
    return jnp.moveaxis(settled, 0, 1)
```

```python
import math

import jax
import jax.numpy as jnp
import numpy as np
from jax import lax
from jax.experimental import pallas as pl
from jax.experimental.pallas import tpu as pltpu
from jax.sharding import PartitionSpec as P

NDIR = 36
NFREQ = 36
SUB = 4

w_plus = 0.4096
w_minus = 3.1605
w_cross = 1.2945
time_step = 0.5

ROW_TILES = 4
STEP = 18


def courant_table():
    d = np.repeat(np.arange(NDIR), NFREQ)
    level = np.tile(np.arange(NFREQ), NDIR)
    angle = 2.0 * math.pi * d / NDIR
    size = 0.7 * 0.93**level
    cos = np.where(d % (NDIR // 2) == NDIR // 4, 0.0, np.cos(angle))
    sin = np.where(d % (NDIR // 2) == 0, 0.0, np.sin(angle))
    along_x, along_y = np.abs(size * cos), np.abs(size * sin)
    return np.stack([1.0 - along_x - along_y, along_x, along_y]).astype(np.float32)


def upwind_pairs(groups, tiles):
    pairs = []
    for c in range(groups):
        east = c * 4 // groups in (0, 3)
        for t in range(tiles):
            to = t + 1 if east else t - 1
            if 0 <= to < tiles:
                pairs.append((c * tiles + t, c * tiles + to))
    return pairs


def propagate_kernel(quarter_ref, coef_ref, own_ref, halo_ref, own_mask_ref, halo_mask_ref, out_ref):
    first = pl.program_id(0) * STEP
    quarter = quarter_ref[0]
    lane = lax.broadcasted_iota(jnp.int32, (8, 128), 1)

    def run(east, north):
        def rows(own, halo):
            both = [halo, own] if east else [own, halo]
            whole = jnp.concatenate(both, axis=0)
            return [whole[:, 128 * i : 128 * (i + 1)] for i in range(ROW_TILES)]

        mask = rows(own_mask_ref[...], halo_mask_ref[...])
        edge = lane == (0 if north else 127)
        base = 4 if east else 0

        def component(k, carry):
            stay, side, row = (coef_ref[i, first + k] for i in range(3))
            field = rows(own_ref[k], halo_ref[k])
            for _ in range(SUB):
                turned = [pltpu.roll(v, 1 if north else 127, 1) for v in field]
                fresh = []
                for i, v in enumerate(field):
                    j = i - 1 if north else i + 1
                    over = turned[j] if 0 <= j < ROW_TILES else 0.0
                    upwind_row = jnp.where(edge, over, turned[i])
                    upwind_col = pltpu.roll(v, 1 if east else 7, 0)
                    fresh.append(mask[i] * (stay * v + side * upwind_col + row * upwind_row))
                field = fresh
            for i, v in enumerate(field):
                for pair in range(2):
                    at = base + 2 * pair
                    out_ref[pair * ROW_TILES + i, k] = v[at : at + 2, :]
            return carry

        lax.fori_loop(0, STEP, component, 0, unroll=3)

    for value, (east, north) in enumerate(((True, True), (False, True), (False, False), (True, False))):
        pl.when(quarter == value)(lambda east=east, north=north: run(east, north))


def settle_kernel(bins_ref, coupling_ref, growth_ref, energy_ref, out_ref, a_ref, b_ref, c_ref, d_ref):
    count = energy_ref.shape[0]
    parts = (a_ref, b_ref, c_ref, d_ref)

    def clear(k, carry):
        for ref in parts:
            ref[k] = jnp.zeros(ref.shape[1:], ref.dtype)
        return carry

    lax.fori_loop(0, count, clear, 0, unroll=16)

    def one(k, carry):
        energy = energy_ref[k]
        scaled = (coupling_ref[k] * time_step) * energy
        total = (1.0 + time_step * growth_ref[k]) * energy
        for mirror in range(2):
            p, q = bins_ref[2 * mirror, k], bins_ref[2 * mirror + 1, k]
            plus, minus = energy_ref[p], energy_ref[q]
            delta = scaled * (energy * (w_plus * plus + w_minus * minus) - (2.0 * w_cross) * plus * minus)
            total = total - 2.0 * delta
            parts[2 * mirror][p] = parts[2 * mirror][p] + delta
            parts[2 * mirror + 1][q] = parts[2 * mirror + 1][q] + delta
        out_ref[k] = total
        return carry

    lax.fori_loop(0, count, one, 0, unroll=8)

    def gather(k, carry):
        out_ref[k] = out_ref[k] + ((a_ref[k] + b_ref[k]) + (c_ref[k] + d_ref[k]))
        return carry

    lax.fori_loop(0, count, gather, 0, unroll=16)


def unpack_kernel(in_ref, out_ref):
    def component(k, carry):
        for i in range(ROW_TILES):
            both = [in_ref[pair * ROW_TILES + i, k] for pair in range(2)]
            out_ref[k, :, 128 * i : 128 * (i + 1)] = jnp.concatenate(both, axis=0)
        return carry

    lax.fori_loop(0, STEP, component, 0, unroll=3)


def per_device(spectrum, sea_mask, quad_bins, coupling, growth):
    comp_dev, width, height = spectrum.shape
    groups, tiles = lax.axis_size("comp"), lax.axis_size("tile")
    mine = lax.axis_index("comp")
    count = comp_dev * groups
    pairs = upwind_pairs(groups, tiles)
    halo_mask = lax.ppermute(sea_mask, ("comp", "tile"), pairs).astype(jnp.float32)
    halo = lax.ppermute(spectrum, ("comp", "tile"), pairs)
    mask = sea_mask.astype(jnp.float32)
    table = lax.dynamic_slice(jnp.asarray(courant_table()), (0, mine * comp_dev), (3, comp_dev))
    quarter = (mine * 4 // groups).reshape(1).astype(jnp.int32)

    smem = pl.BlockSpec(memory_space=pltpu.SMEM)
    whole = pl.BlockSpec((width, height), lambda i: (0, 0))
    wide = pl.BlockSpec((STEP, width, height), lambda i: (i, 0, 0))
    packed = pl.BlockSpec((groups, STEP, 2, 128), lambda i: (0, i, 0, 0))
    pieces = pl.pallas_call(
        propagate_kernel,
        grid=(comp_dev // STEP,),
        in_specs=[smem, smem, wide, wide, whole, whole],
        out_specs=packed,
        out_shape=jax.ShapeDtypeStruct((groups, comp_dev, 2, 128), jnp.float32),
        name="propagate",
    )(quarter, table, spectrum, halo, mask, halo_mask)

    energy = lax.all_to_all(pieces, "comp", split_axis=0, concat_axis=0, tiled=True).reshape(count, 2, 128)
    vmem = pl.BlockSpec(memory_space=pltpu.VMEM)
    fresh = pl.pallas_call(
        settle_kernel,
        in_specs=[smem, smem, smem, vmem],
        out_specs=vmem,
        out_shape=jax.ShapeDtypeStruct((count, 2, 128), jnp.float32),
        scratch_shapes=[pltpu.VMEM((count, 2, 128), jnp.float32)] * 4,
        compiler_params=pltpu.CompilerParams(vmem_limit_bytes=40 << 20),
        name="settle",
    )(quad_bins, coupling, growth, energy)

    back = lax.all_to_all(
        fresh.reshape(groups, comp_dev, 2, 128), "comp", split_axis=0, concat_axis=0, tiled=True
    )
    return pl.pallas_call(
        unpack_kernel,
        grid=(comp_dev // STEP,),
        in_specs=[packed],
        out_specs=wide,
        out_shape=jax.ShapeDtypeStruct((comp_dev, width, height), jnp.float32),
        name="unpack",
    )(back)


def solution(mesh):
    return jax.shard_map(
        per_device,
        mesh=mesh,
        in_specs=(P("comp", "tile", None), P("tile", None), P(), P(), P()),
        out_specs=P("comp", "tile", None),
        check_vma=False,
    )
```

```python
import functools
import math

import jax
import jax.numpy as jnp
import numpy as np
from jax import lax
from jax.experimental import pallas as pl
from jax.experimental.pallas import tpu as pltpu
from jax.sharding import PartitionSpec as P

NDIR = 36
NFREQ = 36
SUB = 4

w_plus = 0.4096
w_minus = 3.1605
w_cross = 1.2945
time_step = 0.5

ROW_TILES = 4
CHUNKS = (84, 78)
TOGETHER = 28
VMEM_LIMIT = 40 << 20


def courant_table():
    d = np.repeat(np.arange(NDIR), NFREQ)
    level = np.tile(np.arange(NFREQ), NDIR)
    angle = 2.0 * math.pi * d / NDIR
    size = 0.7 * 0.93**level
    cos = np.where(d % (NDIR // 2) == NDIR // 4, 0.0, np.cos(angle))
    sin = np.where(d % (NDIR // 2) == 0, 0.0, np.sin(angle))
    along_x, along_y = np.abs(size * cos), np.abs(size * sin)
    return np.stack([1.0 - along_x - along_y, along_x, along_y], axis=1).astype(np.float32)


def upwind_pairs(groups, tiles):
    pairs = []
    for c in range(groups):
        east = c * 4 // groups in (0, 3)
        for t in range(tiles):
            to = t + 1 if east else t - 1
            if 0 <= to < tiles:
                pairs.append((c * tiles + t, c * tiles + to))
    return pairs


def rows_of(size):
    return -(-2 * size // 8) * 8


def pair_of(row):
    return pl.ds(pl.multiple_of(row, 2), 2)


def propagate_kernel(first, quarter_ref, coef_ref, own_ref, halo_ref, own_mask_ref, halo_mask_ref, out_ref):
    size = own_ref.shape[0]
    side_by_side = max(n for n in range(1, TOGETHER + 1) if size % n == 0)
    quarter = quarter_ref[0]
    lane = lax.broadcasted_iota(jnp.int32, (8, 128), 1)
    extra = out_ref.shape[1] - 2 * size
    if extra:
        for piece in range(out_ref.shape[0]):
            out_ref[piece, 2 * size :, :] = jnp.zeros((extra, 128), jnp.float32)

    def run(east, north):
        def rows(own, halo):
            whole = jnp.concatenate([halo, own] if east else [own, halo], axis=0)
            return [whole[:, 128 * i : 128 * (i + 1)] for i in range(ROW_TILES)]

        mask = rows(own_mask_ref[...].astype(jnp.float32), halo_mask_ref[...].astype(jnp.float32))
        edge = lane == (0 if north else 127)
        base = 4 if east else 0

        def several(step, carry):
            which = [step * side_by_side + u for u in range(side_by_side)]
            coefs = [[coef_ref[3 * (first + k) + i] for i in range(3)] for k in which]
            fields = [rows(own_ref[k], halo_ref[k]) for k in which]
            for _ in range(SUB):
                turned = [[pltpu.roll(v, 1 if north else 127, 1) for v in field] for field in fields]
                cols = [[pltpu.roll(v, 1 if east else 7, 0) for v in field] for field in fields]
                fresh = []
                for u, (stay, side, along) in enumerate(coefs):
                    field = []
                    for i in range(ROW_TILES):
                        j = i - 1 if north else i + 1
                        over = turned[u][j] if 0 <= j < ROW_TILES else 0.0
                        upwind_row = jnp.where(edge, over, turned[u][i])
                        field.append(mask[i] * (stay * fields[u][i] + side * cols[u][i] + along * upwind_row))
                    fresh.append(field)
                fields = fresh
            for u, k in enumerate(which):
                for i, v in enumerate(fields[u]):
                    for pair in range(2):
                        at = base + 2 * pair
                        out_ref[pair * ROW_TILES + i, pair_of(2 * k), :] = v[at : at + 2, :]
            return carry

        lax.fori_loop(0, size // side_by_side, several, 0)

    for value, (east, north) in enumerate(((True, True), (False, True), (False, False), (True, False))):
        pl.when(quarter == value)(functools.partial(run, east, north))


def settle_kernel(bins_ref, coupling_ref, growth_ref, *refs):
    pieces, (out_ref, energy_ref, a_ref, b_ref, c_ref, d_ref, sems) = refs[: len(CHUNKS)], refs[len(CHUNKS) :]
    parts = (a_ref, b_ref, c_ref, d_ref)
    total_rows = energy_ref.shape[0]
    groups = pieces[0].shape[0]
    copies = []
    start = 0
    for piece in pieces:
        rows = piece.shape[1]
        for g in range(groups):
            place = energy_ref.at[pl.ds(g * (total_rows // groups) + start, rows), :]
            copies.append(pltpu.make_async_copy(piece.at[g], place, sems.at[len(copies)]))
        start += rows
    for copy in copies:
        copy.start()

    def tile_of(t):
        return pl.ds(pl.multiple_of(8 * t, 8), 8)

    def clear(t, carry):
        for ref in parts:
            ref[tile_of(t), :] = jnp.zeros((8, 128), jnp.float32)
        return carry

    lax.fori_loop(0, total_rows // 8, clear, 0, unroll=4)
    for copy in copies:
        copy.wait()

    def one(k, carry):
        rows = [pair_of(bins_ref[4 * k + j]) for j in range(4)]
        here = pair_of(2 * k)
        energy = energy_ref[here, :]
        scaled = coupling_ref[k] * energy
        total = growth_ref[k] * energy
        for mirror in range(2):
            p, q = rows[2 * mirror], rows[2 * mirror + 1]
            plus, minus = energy_ref[p, :], energy_ref[q, :]
            delta = scaled * (energy * (w_plus * plus + w_minus * minus) - (2.0 * w_cross) * plus * minus)
            total = total - 2.0 * delta
            for ref, row in ((parts[2 * mirror], p), (parts[2 * mirror + 1], q)):
                ref[row, :] = ref[row, :] + delta
        out_ref[here, :] = total
        return carry

    lax.fori_loop(0, total_rows // 2, one, 0, unroll=16)

    def gather(t, carry):
        s = tile_of(t)
        out_ref[s, :] = out_ref[s, :] + ((a_ref[s, :] + b_ref[s, :]) + (c_ref[s, :] + d_ref[s, :]))
        return carry

    lax.fori_loop(0, total_rows // 8, gather, 0, unroll=4)


def unpack_kernel(in_ref, out_ref):
    step_size = 9

    def several(step, carry):
        which = [step * step_size + u for u in range(step_size)]
        both = [
            [[in_ref[pair * ROW_TILES + i, pair_of(2 * k), :] for pair in range(2)] for i in range(ROW_TILES)]
            for k in which
        ]
        for u, k in enumerate(which):
            for i in range(ROW_TILES):
                out_ref[k, :, 128 * i : 128 * (i + 1)] = jnp.concatenate(both[u][i], axis=0)
        return carry

    lax.fori_loop(0, out_ref.shape[0] // step_size, several, 0)


def per_device(spectrum, sea_mask, quad_bins, coupling, growth):
    comp_dev, width, height = spectrum.shape
    groups, tiles = lax.axis_size("comp"), lax.axis_size("tile")
    mine = lax.axis_index("comp")
    count = comp_dev * groups
    group_rows = sum(rows_of(size) for size in CHUNKS)
    pairs = upwind_pairs(groups, tiles)
    table = lax.dynamic_slice(jnp.asarray(courant_table().reshape(-1)), (3 * mine * comp_dev,), (3 * comp_dev,))
    quarter = (mine * 4 // groups).reshape(1).astype(jnp.int32)

    smem = pl.BlockSpec(memory_space=pltpu.SMEM)
    vmem = pl.BlockSpec(memory_space=pltpu.VMEM)
    params = pltpu.CompilerParams(vmem_limit_bytes=VMEM_LIMIT)

    starts = [sum(CHUNKS[:i]) for i in range(len(CHUNKS))]
    owns = [lax.slice_in_dim(spectrum, s, s + n, axis=0) for s, n in zip(starts, CHUNKS)]
    halos = [lax.ppermute(owns[0], ("comp", "tile"), pairs)]
    halo_mask = lax.ppermute(sea_mask, ("comp", "tile"), pairs)
    halos += [lax.ppermute(own, ("comp", "tile"), pairs) for own in owns[1:]]

    spare = group_rows // 2 - comp_dev
    own_rows = np.arange(groups)[:, None] * group_rows + 2 * (comp_dev + np.arange(spare))[None]
    where = 2 * quad_bins.T + (group_rows - 2 * comp_dev) * (quad_bins.T // comp_dev)
    fill = jnp.asarray(np.repeat(own_rows[:, :, None], 4, axis=2).astype(np.int32))
    where = jnp.concatenate([where.reshape(groups, comp_dev, 4), fill], axis=1).reshape(-1)
    pad = lambda v: jnp.pad(v.reshape(groups, comp_dev), ((0, 0), (0, spare))).reshape(-1)
    strength, kept = pad(time_step * coupling), pad(1.0 + time_step * growth)

    pieces = []
    for i, (start, size) in enumerate(zip(starts, CHUNKS)):
        moved = pl.pallas_call(
            functools.partial(propagate_kernel, start),
            in_specs=[smem, smem, vmem, vmem, vmem, vmem],
            out_specs=vmem,
            out_shape=jax.ShapeDtypeStruct((groups, rows_of(size), 128), jnp.float32),
            compiler_params=params,
            cost_estimate=pl.CostEstimate(flops=100 * size * 2048, bytes_accessed=12 * size * 2048, transcendentals=0),
            name=f"propagate_{i}",
        )(quarter, table, owns[i], halos[i], sea_mask, halo_mask)
        pieces.append(lax.all_to_all(moved, "comp", split_axis=0, concat_axis=0, tiled=True))

    total_rows = groups * group_rows
    fresh = pl.pallas_call(
        settle_kernel,
        in_specs=[smem, smem, smem] + [pl.BlockSpec(memory_space=pl.ANY)] * len(CHUNKS),
        out_specs=vmem,
        out_shape=jax.ShapeDtypeStruct((total_rows, 128), jnp.float32),
        scratch_shapes=[pltpu.VMEM((total_rows, 128), jnp.float32)] * 5
        + [pltpu.SemaphoreType.DMA((len(CHUNKS) * groups,))],
        compiler_params=params,
        name="settle",
    )(where, strength, kept, *pieces)

    back = lax.all_to_all(fresh.reshape(groups, group_rows, 128), "comp", split_axis=0, concat_axis=0, tiled=True)
    return pl.pallas_call(
        unpack_kernel,
        in_specs=[vmem],
        out_specs=vmem,
        out_shape=jax.ShapeDtypeStruct((comp_dev, width, height), jnp.float32),
        compiler_params=params,
        name="unpack",
    )(back)


def solution(mesh):
    return jax.shard_map(
        per_device,
        mesh=mesh,
        in_specs=(P("comp", "tile", None), P("tile", None), P(), P(), P()),
        out_specs=P("comp", "tile", None),
        check_vma=False,
    )
```

```python
import functools
import math

import jax
import jax.numpy as jnp
import numpy as np
from jax import lax
from jax.experimental import pallas as pl
from jax.experimental.pallas import tpu as pltpu
from jax.sharding import PartitionSpec as P

NDIR = 36
NFREQ = 36
SUB = 4

w_plus = 0.4096
w_minus = 3.1605
w_cross = 1.2945
time_step = 0.5

ROW_TILES = 4
CHUNKS = (84, 78)
TOGETHER = 28
VMEM_LIMIT = 40 << 20


def courant_table():
    d = np.repeat(np.arange(NDIR), NFREQ)
    level = np.tile(np.arange(NFREQ), NDIR)
    angle = 2.0 * math.pi * d / NDIR
    size = 0.7 * 0.93**level
    cos = np.where(d % (NDIR // 2) == NDIR // 4, 0.0, np.cos(angle))
    sin = np.where(d % (NDIR // 2) == 0, 0.0, np.sin(angle))
    along_x, along_y = np.abs(size * cos), np.abs(size * sin)
    return np.stack([1.0 - along_x - along_y, along_x, along_y], axis=1).astype(np.float32)


def upwind_pairs(groups, tiles):
    pairs = []
    for c in range(groups):
        east = c * 4 // groups in (0, 3)
        for t in range(tiles):
            to = t + 1 if east else t - 1
            if 0 <= to < tiles:
                pairs.append((c * tiles + t, c * tiles + to))
    return pairs


def rows_of(size):
    return -(-2 * size // 8) * 8


def pair_of(row):
    return pl.ds(pl.multiple_of(row, 2), 2)


def propagate_kernel(first, quarter_ref, coef_ref, own_ref, halo_ref, out_ref):
    size = own_ref.shape[0] - 1
    side_by_side = max(n for n in range(1, TOGETHER + 1) if size % n == 0)
    quarter = quarter_ref[0]
    lane = lax.broadcasted_iota(jnp.int32, (8, 128), 1)
    extra = out_ref.shape[1] - 2 * size
    if extra:
        for piece in range(out_ref.shape[0]):
            out_ref[piece, 2 * size :, :] = jnp.zeros((extra, 128), jnp.float32)

    def run(east, north):
        def rows(own, halo):
            whole = jnp.concatenate([halo, own] if east else [own, halo], axis=0)
            return [whole[:, 128 * i : 128 * (i + 1)] for i in range(ROW_TILES)]

        mask = rows(own_ref[size], halo_ref[size])
        edge = lane == (0 if north else 127)
        base = 4 if east else 0

        def several(step, carry):
            which = [step * side_by_side + u for u in range(side_by_side)]
            coefs = [[coef_ref[3 * (first + k) + i] for i in range(3)] for k in which]
            fields = [rows(own_ref[k], halo_ref[k]) for k in which]
            for _ in range(SUB):
                turned = [[pltpu.roll(v, 1 if north else 127, 1) for v in field] for field in fields]
                cols = [[pltpu.roll(v, 1 if east else 7, 0) for v in field] for field in fields]
                fresh = []
                for u, (stay, side, along) in enumerate(coefs):
                    field = []
                    for i in range(ROW_TILES):
                        j = i - 1 if north else i + 1
                        over = turned[u][j] if 0 <= j < ROW_TILES else 0.0
                        upwind_row = jnp.where(edge, over, turned[u][i])
                        field.append(mask[i] * (stay * fields[u][i] + side * cols[u][i] + along * upwind_row))
                    fresh.append(field)
                fields = fresh
            for u, k in enumerate(which):
                for i, v in enumerate(fields[u]):
                    for pair in range(2):
                        at = base + 2 * pair
                        out_ref[pair * ROW_TILES + i, pair_of(2 * k), :] = v[at : at + 2, :]
            return carry

        lax.fori_loop(0, size // side_by_side, several, 0)

    for value, (east, north) in enumerate(((True, True), (False, True), (False, False), (True, False))):
        pl.when(quarter == value)(functools.partial(run, east, north))


def settle_kernel(bins_ref, coupling_ref, growth_ref, *refs):
    pieces, (out_ref, energy_ref, a_ref, b_ref, c_ref, d_ref, sems) = refs[: len(CHUNKS)], refs[len(CHUNKS) :]
    parts = (a_ref, b_ref, c_ref, d_ref)
    total_rows = energy_ref.shape[0]
    groups = pieces[0].shape[0]
    copies = []
    start = 0
    for piece in pieces:
        rows = piece.shape[1]
        for g in range(groups):
            place = energy_ref.at[pl.ds(g * (total_rows // groups) + start, rows), :]
            copies.append(pltpu.make_async_copy(piece.at[g], place, sems.at[len(copies)]))
        start += rows
    for copy in copies:
        copy.start()

    def tile_of(t):
        return pl.ds(pl.multiple_of(8 * t, 8), 8)

    def clear(t, carry):
        for ref in parts:
            ref[tile_of(t), :] = jnp.zeros((8, 128), jnp.float32)
        return carry

    lax.fori_loop(0, total_rows // 8, clear, 0, unroll=4)
    for copy in copies:
        copy.wait()

    def one(k, carry):
        rows = [pair_of(bins_ref[4 * k + j]) for j in range(4)]
        here = pair_of(2 * k)
        energy = energy_ref[here, :]
        scaled = coupling_ref[k] * energy
        total = growth_ref[k] * energy
        for mirror in range(2):
            p, q = rows[2 * mirror], rows[2 * mirror + 1]
            plus, minus = energy_ref[p, :], energy_ref[q, :]
            delta = scaled * (energy * (w_plus * plus + w_minus * minus) - (2.0 * w_cross) * plus * minus)
            total = total - 2.0 * delta
            for ref, row in ((parts[2 * mirror], p), (parts[2 * mirror + 1], q)):
                ref[row, :] = ref[row, :] + delta
        out_ref[here, :] = total
        return carry

    lax.fori_loop(0, total_rows // 2, one, 0, unroll=16)

    def gather(t, carry):
        s = tile_of(t)
        out_ref[s, :] = out_ref[s, :] + ((a_ref[s, :] + b_ref[s, :]) + (c_ref[s, :] + d_ref[s, :]))
        return carry

    lax.fori_loop(0, total_rows // 8, gather, 0, unroll=4)


def unpack_kernel(in_ref, out_ref):
    step_size = 9

    def several(step, carry):
        which = [step * step_size + u for u in range(step_size)]
        both = [
            [[in_ref[pair * ROW_TILES + i, pair_of(2 * k), :] for pair in range(2)] for i in range(ROW_TILES)]
            for k in which
        ]
        for u, k in enumerate(which):
            for i in range(ROW_TILES):
                out_ref[k, :, 128 * i : 128 * (i + 1)] = jnp.concatenate(both[u][i], axis=0)
        return carry

    lax.fori_loop(0, out_ref.shape[0] // step_size, several, 0)


def per_device(spectrum, sea_mask, quad_bins, coupling, growth):
    comp_dev, width, height = spectrum.shape
    groups, tiles = lax.axis_size("comp"), lax.axis_size("tile")
    mine = lax.axis_index("comp")
    count = comp_dev * groups
    group_rows = sum(rows_of(size) for size in CHUNKS)
    pairs = upwind_pairs(groups, tiles)
    table = lax.dynamic_slice(jnp.asarray(courant_table().reshape(-1)), (3 * mine * comp_dev,), (3 * comp_dev,))
    quarter = (mine * 4 // groups).reshape(1).astype(jnp.int32)

    smem = pl.BlockSpec(memory_space=pltpu.SMEM)
    vmem = pl.BlockSpec(memory_space=pltpu.VMEM)
    params = pltpu.CompilerParams(vmem_limit_bytes=VMEM_LIMIT)

    starts = [sum(CHUNKS[:i]) for i in range(len(CHUNKS))]
    mask = sea_mask.astype(jnp.float32)[None]
    owns = [
        jnp.concatenate([lax.slice_in_dim(spectrum, s, s + n, axis=0), mask], axis=0) for s, n in zip(starts, CHUNKS)
    ]
    halos = [lax.ppermute(own, ("comp", "tile"), pairs) for own in owns]

    spare = group_rows // 2 - comp_dev
    own_rows = np.arange(groups)[:, None] * group_rows + 2 * (comp_dev + np.arange(spare))[None]
    where = 2 * quad_bins.T + (group_rows - 2 * comp_dev) * (quad_bins.T // comp_dev)
    fill = jnp.asarray(np.repeat(own_rows[:, :, None], 4, axis=2).astype(np.int32))
    where = jnp.concatenate([where.reshape(groups, comp_dev, 4), fill], axis=1).reshape(-1)
    pad = lambda v: jnp.pad(v.reshape(groups, comp_dev), ((0, 0), (0, spare))).reshape(-1)
    strength, kept = pad(time_step * coupling), pad(1.0 + time_step * growth)

    pieces = []
    for i, (start, size) in enumerate(zip(starts, CHUNKS)):
        moved = pl.pallas_call(
            functools.partial(propagate_kernel, start),
            in_specs=[smem, smem, vmem, vmem],
            out_specs=vmem,
            out_shape=jax.ShapeDtypeStruct((groups, rows_of(size), 128), jnp.float32),
            compiler_params=params,
            cost_estimate=pl.CostEstimate(flops=100 * size * 2048, bytes_accessed=12 * size * 2048, transcendentals=0),
            name=f"propagate_{i}",
        )(quarter, table, owns[i], halos[i])
        pieces.append(lax.all_to_all(moved, "comp", split_axis=0, concat_axis=0, tiled=True))

    total_rows = groups * group_rows
    fresh = pl.pallas_call(
        settle_kernel,
        in_specs=[smem, smem, smem] + [pl.BlockSpec(memory_space=pl.ANY)] * len(CHUNKS),
        out_specs=vmem,
        out_shape=jax.ShapeDtypeStruct((total_rows, 128), jnp.float32),
        scratch_shapes=[pltpu.VMEM((total_rows, 128), jnp.float32)] * 5
        + [pltpu.SemaphoreType.DMA((len(CHUNKS) * groups,))],
        compiler_params=params,
        name="settle",
    )(where, strength, kept, *pieces)

    back = lax.all_to_all(fresh.reshape(groups, group_rows, 128), "comp", split_axis=0, concat_axis=0, tiled=True)
    return pl.pallas_call(
        unpack_kernel,
        in_specs=[vmem],
        out_specs=vmem,
        out_shape=jax.ShapeDtypeStruct((comp_dev, width, height), jnp.float32),
        compiler_params=params,
        name="unpack",
    )(back)


def solution(mesh):
    return jax.shard_map(
        per_device,
        mesh=mesh,
        in_specs=(P("comp", "tile", None), P("tile", None), P(), P(), P()),
        out_specs=P("comp", "tile", None),
        check_vma=False,
    )
```

```python
import functools
import math

import jax
import jax.numpy as jnp
import numpy as np
from jax import lax
from jax.experimental import pallas as pl
from jax.experimental.pallas import tpu as pltpu
from jax.sharding import PartitionSpec as P

NDIR = 36
NFREQ = 36
SUB = 4

w_plus = 0.4096
w_minus = 3.1605
w_cross = 1.2945
time_step = 0.5

ROW_TILES = 4
CHUNKS = (96, 66)
TOGETHER = 28
VMEM_LIMIT = 40 << 20


def courant_table():
    d = np.repeat(np.arange(NDIR), NFREQ)
    level = np.tile(np.arange(NFREQ), NDIR)
    angle = 2.0 * math.pi * d / NDIR
    size = 0.7 * 0.93**level
    cos = np.where(d % (NDIR // 2) == NDIR // 4, 0.0, np.cos(angle))
    sin = np.where(d % (NDIR // 2) == 0, 0.0, np.sin(angle))
    along_x, along_y = np.abs(size * cos), np.abs(size * sin)
    return np.stack([1.0 - along_x - along_y, along_x, along_y], axis=1).astype(np.float32)


def upwind_pairs(groups, tiles):
    pairs = []
    for c in range(groups):
        east = c * 4 // groups in (0, 3)
        for t in range(tiles):
            to = t + 1 if east else t - 1
            if 0 <= to < tiles:
                pairs.append((c * tiles + t, c * tiles + to))
    return pairs


def rows_of(size):
    return -(-2 * size // 8) * 8


def pair_of(row):
    return pl.ds(pl.multiple_of(row, 2), 2)


def propagate_kernel(first, quarter_ref, coef_ref, own_ref, halo_ref, out_ref):
    size = own_ref.shape[0] - 1
    side_by_side = max(n for n in range(1, TOGETHER + 1) if size % n == 0)
    quarter = quarter_ref[0]
    lane = lax.broadcasted_iota(jnp.int32, (8, 128), 1)
    extra = out_ref.shape[1] - 2 * size
    if extra:
        for piece in range(out_ref.shape[0]):
            out_ref[piece, 2 * size :, :] = jnp.zeros((extra, 128), jnp.float32)

    def run(east, north):
        def rows(own, halo):
            whole = jnp.concatenate([halo, own] if east else [own, halo], axis=0)
            return [whole[:, 128 * i : 128 * (i + 1)] for i in range(ROW_TILES)]

        mask = rows(own_ref[size], halo_ref[size])
        edge = lane == (0 if north else 127)
        base = 4 if east else 0

        def several(step, carry):
            which = [step * side_by_side + u for u in range(side_by_side)]
            coefs = [[coef_ref[3 * (first + k) + i] for i in range(3)] for k in which]
            fields = [rows(own_ref[k], halo_ref[k]) for k in which]
            for _ in range(SUB):
                turned = [[pltpu.roll(v, 1 if north else 127, 1) for v in field] for field in fields]
                cols = [[pltpu.roll(v, 1 if east else 7, 0) for v in field] for field in fields]
                fresh = []
                for u, (stay, side, along) in enumerate(coefs):
                    field = []
                    for i in range(ROW_TILES):
                        j = i - 1 if north else i + 1
                        over = turned[u][j] if 0 <= j < ROW_TILES else 0.0
                        upwind_row = jnp.where(edge, over, turned[u][i])
                        field.append(mask[i] * (stay * fields[u][i] + side * cols[u][i] + along * upwind_row))
                    fresh.append(field)
                fields = fresh
            for u, k in enumerate(which):
                for i, v in enumerate(fields[u]):
                    for pair in range(2):
                        at = base + 2 * pair
                        out_ref[pair * ROW_TILES + i, pair_of(2 * k), :] = v[at : at + 2, :]
            return carry

        lax.fori_loop(0, size // side_by_side, several, 0)

    for value, (east, north) in enumerate(((True, True), (False, True), (False, False), (True, False))):
        pl.when(quarter == value)(functools.partial(run, east, north))


def settle_kernel(bins_ref, strength_ref, kept_ref, *refs):
    pieces = refs[: len(CHUNKS)]
    out_ref, energy_ref, *parts = refs[len(CHUNKS) :]
    total_rows = energy_ref.shape[0]
    groups = pieces[0].shape[0]

    def tile_of(t):
        return pl.ds(pl.multiple_of(8 * t, 8), 8)

    def take(piece, shift, g, carry):
        for t in range(piece.shape[1] // 8):
            here = pl.ds(pl.multiple_of(g * (total_rows // groups) + shift + 8 * t, 8), 8)
            energy_ref[here, :] = piece[g, 8 * t : 8 * t + 8, :]
            for ref in parts:
                ref[here, :] = jnp.zeros((8, 128), jnp.float32)
        return carry

    shift = 0
    for piece in pieces:
        lax.fori_loop(0, groups, functools.partial(take, piece, shift), 0)
        shift += piece.shape[1]

    def one(k, carry):
        rows = [pair_of(bins_ref[4 * k + j]) for j in range(4)]
        here = pair_of(2 * k)
        energy = energy_ref[here, :]
        scaled = strength_ref[k] * energy
        cross, squared = (2.0 * w_cross) * scaled, scaled * energy
        squared_plus, squared_minus = w_plus * squared, w_minus * squared
        deltas = []
        for mirror in range(2):
            plus, minus = (energy_ref[row, :] for row in rows[2 * mirror : 2 * mirror + 2])
            deltas.append(minus * (squared_minus - cross * plus) + squared_plus * plus)
        for j, row in enumerate(rows):
            parts[j][row, :] = parts[j][row, :] + deltas[j // 2]
        out_ref[here, :] = kept_ref[k] * energy - 2.0 * (deltas[0] + deltas[1])
        return carry

    lax.fori_loop(0, total_rows // 2, one, 0, unroll=16)

    def gather(t, carry):
        s = tile_of(t)
        a, b, c, d = (ref[s, :] for ref in parts)
        out_ref[s, :] = out_ref[s, :] + ((a + b) + (c + d))
        return carry

    lax.fori_loop(0, total_rows // 8, gather, 0, unroll=8)


def unpack_kernel(in_ref, out_ref):
    step_size = 9

    def several(step, carry):
        which = [step * step_size + u for u in range(step_size)]
        both = [
            [[in_ref[pair * ROW_TILES + i, pair_of(2 * k), :] for pair in range(2)] for i in range(ROW_TILES)]
            for k in which
        ]
        for u, k in enumerate(which):
            for i in range(ROW_TILES):
                out_ref[k, :, 128 * i : 128 * (i + 1)] = jnp.concatenate(both[u][i], axis=0)
        return carry

    lax.fori_loop(0, out_ref.shape[0] // step_size, several, 0)


def per_device(spectrum, sea_mask, quad_bins, coupling, growth):
    comp_dev, width, height = spectrum.shape
    groups, tiles = lax.axis_size("comp"), lax.axis_size("tile")
    mine = lax.axis_index("comp")
    count = comp_dev * groups
    group_rows = sum(rows_of(size) for size in CHUNKS)
    pairs = upwind_pairs(groups, tiles)
    table = lax.dynamic_slice(jnp.asarray(courant_table().reshape(-1)), (3 * mine * comp_dev,), (3 * comp_dev,))
    quarter = (mine * 4 // groups).reshape(1).astype(jnp.int32)

    smem = pl.BlockSpec(memory_space=pltpu.SMEM)
    vmem = pl.BlockSpec(memory_space=pltpu.VMEM)
    params = pltpu.CompilerParams(vmem_limit_bytes=VMEM_LIMIT)

    starts = [sum(CHUNKS[:i]) for i in range(len(CHUNKS))]
    mask = sea_mask.astype(jnp.float32)[None]
    owns = [
        jnp.concatenate([lax.slice_in_dim(spectrum, s, s + n, axis=0), mask], axis=0) for s, n in zip(starts, CHUNKS)
    ]
    halos = [lax.ppermute(own, ("comp", "tile"), pairs) for own in owns]

    spare = group_rows // 2 - comp_dev
    own_rows = np.arange(groups)[:, None] * group_rows + 2 * (comp_dev + np.arange(spare))[None]
    where = 2 * quad_bins.T + (group_rows - 2 * comp_dev) * (quad_bins.T // comp_dev)
    fill = jnp.asarray(np.repeat(own_rows[:, :, None], 4, axis=2).astype(np.int32))
    where = jnp.concatenate([where.reshape(groups, comp_dev, 4), fill], axis=1).reshape(-1)

    pad = lambda v: jnp.pad(v.reshape(groups, comp_dev), ((0, 0), (0, spare))).reshape(-1)
    strength, kept = pad(time_step * coupling), pad(1.0 + time_step * growth)

    pieces = []
    for i, (start, size) in enumerate(zip(starts, CHUNKS)):
        moved = pl.pallas_call(
            functools.partial(propagate_kernel, start),
            in_specs=[smem, smem, vmem, vmem],
            out_specs=vmem,
            out_shape=jax.ShapeDtypeStruct((groups, rows_of(size), 128), jnp.float32),
            compiler_params=params,
            cost_estimate=pl.CostEstimate(flops=100 * size * 2048, bytes_accessed=12 * size * 2048, transcendentals=0),
            name=f"propagate_{i}",
        )(quarter, table, owns[i], halos[i])
        pieces.append(lax.all_to_all(moved, "comp", split_axis=0, concat_axis=0, tiled=True))

    total_rows = groups * group_rows
    fresh = pl.pallas_call(
        settle_kernel,
        in_specs=[smem, smem, smem] + [vmem] * len(CHUNKS),
        out_specs=vmem,
        out_shape=jax.ShapeDtypeStruct((total_rows, 128), jnp.float32),
        scratch_shapes=[pltpu.VMEM((total_rows, 128), jnp.float32)] * 5,
        compiler_params=params,
        name="settle",
    )(where, strength, kept, *pieces)

    back = lax.all_to_all(fresh.reshape(groups, group_rows, 128), "comp", split_axis=0, concat_axis=0, tiled=True)
    return pl.pallas_call(
        unpack_kernel,
        in_specs=[vmem],
        out_specs=vmem,
        out_shape=jax.ShapeDtypeStruct((comp_dev, width, height), jnp.float32),
        compiler_params=params,
        name="unpack",
    )(back)


def solution(mesh):
    return jax.shard_map(
        per_device,
        mesh=mesh,
        in_specs=(P("comp", "tile", None), P("tile", None), P(), P(), P()),
        out_specs=P("comp", "tile", None),
        check_vma=False,
    )
```

```python
import functools
import math

import jax
import jax.numpy as jnp
import numpy as np
from jax import lax
from jax.experimental import pallas as pl
from jax.experimental.pallas import tpu as pltpu
from jax.sharding import PartitionSpec as P

NDIR = 36
NFREQ = 36
SUB = 4

w_plus = 0.4096
w_minus = 3.1605
w_cross = 1.2945
time_step = 0.5

ROW_TILES = 4
CHUNKS = (96, 66)
TOGETHER = 28
VMEM_LIMIT = 40 << 20
COST = 200_000


def courant_table():
    d = np.repeat(np.arange(NDIR), NFREQ)
    level = np.tile(np.arange(NFREQ), NDIR)
    angle = 2.0 * math.pi * d / NDIR
    size = 0.7 * 0.93**level
    cos = np.where(d % (NDIR // 2) == NDIR // 4, 0.0, np.cos(angle))
    sin = np.where(d % (NDIR // 2) == 0, 0.0, np.sin(angle))
    along_x, along_y = np.abs(size * cos), np.abs(size * sin)
    return np.stack([1.0 - along_x - along_y, along_x, along_y], axis=1).astype(np.float32)


def is_east(c, groups):
    return c * 4 // groups in (0, 3)


def halo_pairs(groups, tiles, flip):
    pairs = []
    for c in range(groups):
        step = 1 if (c % 2 == 0) != flip else -1
        pairs += [(c * tiles + t, c * tiles + (t + step) % tiles) for t in range(tiles)]
    return pairs


def window_groups(groups, tiles):
    return [[c * tiles + (t if is_east(c, groups) else (t + 1) % tiles) for c in range(groups)] for t in range(tiles)]


def holders(groups):
    east = [c for c in range(groups) if is_east(c, groups)]
    return east, [c for c in range(groups) if c not in east]


def rows_of(size):
    return -(-2 * size // 8) * 8


def pair_of(row):
    return pl.ds(pl.multiple_of(row, 2), 2)


def propagate_kernel(first, place_ref, coef_ref, own_ref, one_ref, other_ref, *refs):
    *before_refs, out_ref = refs
    size = own_ref.shape[0] - 1
    side_by_side = max(n for n in range(1, TOGETHER + 1) if size % n == 0)
    quarter, swapped, at_start, at_end = (place_ref[i] for i in range(4))
    swapped = swapped == 1
    slots = holders(out_ref.shape[0])
    lane = lax.broadcasted_iota(jnp.int32, (8, 128), 1)
    column = lax.broadcasted_iota(jnp.int32, (8, 128), 0)
    extra = out_ref.shape[1] - 2 * (first + size)
    for piece in range(out_ref.shape[0]):
        for ref in before_refs:
            out_ref[piece, : 2 * first, :] = ref[piece]
        if extra:
            out_ref[piece, 2 * (first + size) :, :] = jnp.zeros((extra, 128), jnp.float32)

    def run(east, north):
        def rows(k):
            one, other = one_ref[k], other_ref[k]
            before, after = jnp.where(swapped, other, one), jnp.where(swapped, one, other)
            whole = jnp.concatenate([before, own_ref[k], after], axis=0)
            return [whole[:, 128 * i : 128 * (i + 1)] for i in range(ROW_TILES)]

        mask = rows(size)
        closed = jnp.where(at_start == 1, 2 if east else 1, jnp.where(at_end == 1, 6 if east else 5, -1))
        open_side = jnp.where(column == closed, 0.0, 1.0)
        edge = lane == (0 if north else 127)
        base = 4 if east else 0

        def several(step, carry):
            which = [step * side_by_side + u for u in range(side_by_side)]
            coefs = [[coef_ref[3 * (first + k) + i] for i in range(3)] for k in which]
            fields = [rows(k) for k in which]
            sides = [side * open_side for _, side, _ in coefs]
            for _ in range(SUB):
                turned = [[pltpu.roll(v, 1 if north else 127, 1) for v in field] for field in fields]
                cols = [[pltpu.roll(v, 1 if east else 7, 0) for v in field] for field in fields]
                fresh = []
                for u, (stay, _, along) in enumerate(coefs):
                    field = []
                    for i in range(ROW_TILES):
                        j = i - 1 if north else i + 1
                        over = turned[u][j] if 0 <= j < ROW_TILES else 0.0
                        upwind_row = jnp.where(edge, over, turned[u][i])
                        field.append(mask[i] * (stay * fields[u][i] + sides[u] * cols[u][i] + along * upwind_row))
                    fresh.append(field)
                fields = fresh
            for u, k in enumerate(which):
                for i, v in enumerate(fields[u]):
                    for pair in range(2):
                        at = base + 2 * pair
                        out_ref[slots[pair][i], pair_of(2 * (first + k)), :] = v[at : at + 2, :]
            return carry

        lax.fori_loop(0, size // side_by_side, several, 0)

    for value, (east, north) in enumerate(((True, True), (False, True), (False, False), (True, False))):
        pl.when(quarter == value)(functools.partial(run, east, north))


def settle_kernel(bins_ref, strength_ref, kept_ref, energy_ref, out_ref, *parts):
    total_rows = energy_ref.shape[0]

    def tile_of(t):
        return pl.ds(pl.multiple_of(8 * t, 8), 8)

    def clear(t, carry):
        for ref in parts:
            ref[tile_of(t), :] = jnp.zeros((8, 128), jnp.float32)
        return carry

    lax.fori_loop(0, total_rows // 8, clear, 0, unroll=8)

    def one(k, carry):
        rows = [pair_of(bins_ref[4 * k + j]) for j in range(4)]
        here = pair_of(2 * k)
        energy = energy_ref[here, :]
        scaled = strength_ref[k] * energy
        cross, squared = (2.0 * w_cross) * scaled, scaled * energy
        squared_plus, squared_minus = w_plus * squared, w_minus * squared
        deltas = []
        for mirror in range(2):
            plus, minus = (energy_ref[row, :] for row in rows[2 * mirror : 2 * mirror + 2])
            deltas.append(minus * (squared_minus - cross * plus) + squared_plus * plus)
        for j, row in enumerate(rows):
            parts[j][row, :] = parts[j][row, :] + deltas[j // 2]
        out_ref[here, :] = kept_ref[k] * energy - 2.0 * (deltas[0] + deltas[1])
        return carry

    lax.fori_loop(0, total_rows // 2, one, 0, unroll=16)

    def gather(t, carry):
        s = tile_of(t)
        a, b, c, d = (ref[s, :] for ref in parts)
        out_ref[s, :] = out_ref[s, :] + ((a + b) + (c + d))
        return carry

    lax.fori_loop(0, total_rows // 8, gather, 0, unroll=8)


def unpack_kernel(in_ref, out_ref):
    step_size = 9
    slots = holders(in_ref.shape[0])[::-1]

    def several(step, carry):
        which = [step * step_size + u for u in range(step_size)]
        both = [
            [[in_ref[slots[pair][i], pair_of(2 * k), :] for pair in range(2)] for i in range(ROW_TILES)]
            for k in which
        ]
        for u, k in enumerate(which):
            for i in range(ROW_TILES):
                out_ref[k, :, 128 * i : 128 * (i + 1)] = jnp.concatenate(both[u][i], axis=0)
        return carry

    lax.fori_loop(0, out_ref.shape[0] // step_size, several, 0)


def per_device(spectrum, sea_mask, quad_bins, coupling, growth):
    comp_dev, width, height = spectrum.shape
    groups, tiles = lax.axis_size("comp"), lax.axis_size("tile")
    mine = lax.axis_index("comp")
    count = comp_dev * groups
    group_rows = rows_of(comp_dev)
    table = lax.dynamic_slice(jnp.asarray(courant_table().reshape(-1)), (3 * mine * comp_dev,), (3 * comp_dev,))
    tile = lax.axis_index("tile")
    odd = mine % 2 == 1
    place = jnp.stack([mine * 4 // groups, mine % 2, tile == 0, tile == tiles - 1]).astype(jnp.int32)

    smem = pl.BlockSpec(memory_space=pltpu.SMEM)
    vmem = pl.BlockSpec(memory_space=pltpu.VMEM)
    params = pltpu.CompilerParams(vmem_limit_bytes=VMEM_LIMIT)

    starts = [sum(CHUNKS[:i]) for i in range(len(CHUNKS))]
    mask = sea_mask.astype(jnp.float32)[None]
    owns = [
        jnp.concatenate([lax.slice_in_dim(spectrum, s, s + n, axis=0), mask], axis=0) for s, n in zip(starts, CHUNKS)
    ]
    half = width // 2
    halos = []
    for own in owns:
        start, end = own[:, :half], own[:, width - half :]
        one = lax.ppermute(jnp.where(odd, start, end), ("comp", "tile"), halo_pairs(groups, tiles, False))
        other = lax.ppermute(jnp.where(odd, end, start), ("comp", "tile"), halo_pairs(groups, tiles, True))
        halos.append((one, other))
    windows = window_groups(groups, tiles)

    spare = group_rows // 2 - comp_dev
    own_rows = np.arange(groups)[:, None] * group_rows + 2 * (comp_dev + np.arange(spare))[None]
    where = 2 * quad_bins.T + (group_rows - 2 * comp_dev) * (quad_bins.T // comp_dev)
    fill = jnp.asarray(np.repeat(own_rows[:, :, None], 4, axis=2).astype(np.int32))
    where = jnp.concatenate([where.reshape(groups, comp_dev, 4), fill], axis=1).reshape(-1)
    pad = lambda v: jnp.pad(v.reshape(groups, comp_dev), ((0, 0), (0, spare))).reshape(-1)
    strength, kept = pad(time_step * coupling), pad(1.0 + time_step * growth)

    moved = []
    for i, (start, size) in enumerate(zip(starts, CHUNKS)):
        moved = [
            pl.pallas_call(
                functools.partial(propagate_kernel, start),
                in_specs=[smem, smem] + [vmem] * (3 + len(moved)),
                out_specs=vmem,
                out_shape=jax.ShapeDtypeStruct((groups, rows_of(start + size), 128), jnp.float32),
                compiler_params=params,
                cost_estimate=pl.CostEstimate(flops=COST * size, bytes_accessed=16384 * size, transcendentals=0),
                name=f"propagate_{i}",
            )(place, table, owns[i], *halos[i], *moved)
        ]
    energy = lax.all_to_all(
        moved[0], ("comp", "tile"), split_axis=0, concat_axis=0, tiled=True, axis_index_groups=windows
    )

    total_rows = groups * group_rows
    fresh = pl.pallas_call(
        settle_kernel,
        in_specs=[smem, smem, smem, vmem],
        out_specs=vmem,
        out_shape=jax.ShapeDtypeStruct((total_rows, 128), jnp.float32),
        scratch_shapes=[pltpu.VMEM((total_rows, 128), jnp.float32)] * 4,
        compiler_params=params,
        name="settle",
    )(where, strength, kept, energy.reshape(total_rows, 128))

    back = lax.all_to_all(fresh.reshape(groups, group_rows, 128), "comp", split_axis=0, concat_axis=0, tiled=True)
    return pl.pallas_call(
        unpack_kernel,
        in_specs=[vmem],
        out_specs=vmem,
        out_shape=jax.ShapeDtypeStruct((comp_dev, width, height), jnp.float32),
        compiler_params=params,
        name="unpack",
    )(back)


def solution(mesh):
    return jax.shard_map(
        per_device,
        mesh=mesh,
        in_specs=(P("comp", "tile", None), P("tile", None), P(), P(), P()),
        out_specs=P("comp", "tile", None),
        check_vma=False,
    )
```

```python
import functools
import math

import jax
import jax.numpy as jnp
import numpy as np
from jax import lax
from jax.experimental import pallas as pl
from jax.experimental.pallas import tpu as pltpu
from jax.sharding import PartitionSpec as P

NDIR = 36
NFREQ = 36
SUB = 4

w_plus = 0.4096
w_minus = 3.1605
w_cross = 1.2945
time_step = 0.5

ROW_TILES = 4
CHUNKS = (162,)
TOGETHER = 28
VMEM_LIMIT = 40 << 20
COST = 200_000


def courant_table():
    d = np.repeat(np.arange(NDIR), NFREQ)
    level = np.tile(np.arange(NFREQ), NDIR)
    angle = 2.0 * math.pi * d / NDIR
    size = 0.7 * 0.93**level
    cos = np.where(d % (NDIR // 2) == NDIR // 4, 0.0, np.cos(angle))
    sin = np.where(d % (NDIR // 2) == 0, 0.0, np.sin(angle))
    along_x, along_y = np.abs(size * cos), np.abs(size * sin)
    return np.stack([1.0 - along_x - along_y, along_x, along_y], axis=1).astype(np.float32)


def is_east(c, groups):
    return c * 4 // groups in (0, 3)


def halo_pairs(groups, tiles, flip):
    pairs = []
    for c in range(groups):
        step = 1 if (c % 2 == 0) != flip else -1
        pairs += [(c * tiles + t, c * tiles + (t + step) % tiles) for t in range(tiles)]
    return pairs


def window_groups(groups, tiles):
    return [[c * tiles + (t if is_east(c, groups) else (t + 1) % tiles) for c in range(groups)] for t in range(tiles)]


def holders(groups):
    east = [c for c in range(groups) if is_east(c, groups)]
    return east, [c for c in range(groups) if c not in east]


def rows_of(size):
    return -(-2 * size // 8) * 8


def pair_of(row):
    return pl.ds(pl.multiple_of(row, 2), 2)


def propagate_kernel(first, place_ref, coef_ref, own_ref, one_ref, other_ref, *refs):
    *before_refs, out_ref = refs
    size = own_ref.shape[0] - 1
    side_by_side = max(n for n in range(1, TOGETHER + 1) if size % n == 0)
    quarter, swapped, at_start, at_end = (place_ref[i] for i in range(4))
    swapped = swapped == 1
    slots = holders(out_ref.shape[0])
    lane = lax.broadcasted_iota(jnp.int32, (8, 128), 1)
    column = lax.broadcasted_iota(jnp.int32, (8, 128), 0)
    extra = out_ref.shape[1] - 2 * (first + size)
    for piece in range(out_ref.shape[0]):
        for ref in before_refs:
            out_ref[piece, : 2 * first, :] = ref[piece]
        if extra:
            out_ref[piece, 2 * (first + size) :, :] = jnp.zeros((extra, 128), jnp.float32)

    def run(east, north):
        def rows(k):
            one, other = one_ref[k], other_ref[k]
            before, after = jnp.where(swapped, other, one), jnp.where(swapped, one, other)
            whole = jnp.concatenate([before, own_ref[k], after], axis=0)
            return [whole[:, 128 * i : 128 * (i + 1)] for i in range(ROW_TILES)]

        mask = rows(size)
        closed = jnp.where(at_start == 1, 2 if east else 1, jnp.where(at_end == 1, 6 if east else 5, -1))
        open_side = jnp.where(column == closed, 0.0, 1.0)
        edge = lane == (0 if north else 127)
        base = 4 if east else 0

        def several(step, carry):
            which = [step * side_by_side + u for u in range(side_by_side)]
            coefs = [[coef_ref[3 * (first + k) + i] for i in range(3)] for k in which]
            fields = [rows(k) for k in which]
            sides = [side * open_side for _, side, _ in coefs]
            for _ in range(SUB):
                turned = [[pltpu.roll(v, 1 if north else 127, 1) for v in field] for field in fields]
                cols = [[pltpu.roll(v, 1 if east else 7, 0) for v in field] for field in fields]
                fresh = []
                for u, (stay, _, along) in enumerate(coefs):
                    field = []
                    for i in range(ROW_TILES):
                        j = i - 1 if north else i + 1
                        over = turned[u][j] if 0 <= j < ROW_TILES else 0.0
                        upwind_row = jnp.where(edge, over, turned[u][i])
                        field.append(mask[i] * (stay * fields[u][i] + sides[u] * cols[u][i] + along * upwind_row))
                    fresh.append(field)
                fields = fresh
            for u, k in enumerate(which):
                for i, v in enumerate(fields[u]):
                    for pair in range(2):
                        at = base + 2 * pair
                        out_ref[slots[pair][i], pair_of(2 * (first + k)), :] = v[at : at + 2, :]
            return carry

        lax.fori_loop(0, size // side_by_side, several, 0)

    for value, (east, north) in enumerate(((True, True), (False, True), (False, False), (True, False))):
        pl.when(quarter == value)(functools.partial(run, east, north))


def settle_kernel(bins_ref, strength_ref, kept_ref, energy_ref, out_ref, *parts):
    total_rows = energy_ref.shape[0]

    def tile_of(t):
        return pl.ds(pl.multiple_of(8 * t, 8), 8)

    def clear(t, carry):
        for ref in parts:
            ref[tile_of(t), :] = jnp.zeros((8, 128), jnp.float32)
        return carry

    lax.fori_loop(0, total_rows // 8, clear, 0, unroll=8)

    def one(k, carry):
        rows = [pair_of(bins_ref[4 * k + j]) for j in range(4)]
        here = pair_of(2 * k)
        energy = energy_ref[here, :]
        scaled = strength_ref[k] * energy
        cross, squared = (2.0 * w_cross) * scaled, scaled * energy
        squared_plus, squared_minus = w_plus * squared, w_minus * squared
        deltas = []
        for mirror in range(2):
            plus, minus = (energy_ref[row, :] for row in rows[2 * mirror : 2 * mirror + 2])
            deltas.append(minus * (squared_minus - cross * plus) + squared_plus * plus)
        for j, row in enumerate(rows):
            parts[j][row, :] = parts[j][row, :] + deltas[j // 2]
        out_ref[here, :] = kept_ref[k] * energy - 2.0 * (deltas[0] + deltas[1])
        return carry

    lax.fori_loop(0, total_rows // 2, one, 0, unroll=16)

    def gather(t, carry):
        s = tile_of(t)
        a, b, c, d = (ref[s, :] for ref in parts)
        out_ref[s, :] = out_ref[s, :] + ((a + b) + (c + d))
        return carry

    lax.fori_loop(0, total_rows // 8, gather, 0, unroll=8)


def unpack_kernel(in_ref, out_ref):
    step_size = 9
    slots = holders(in_ref.shape[0])[::-1]

    def several(step, carry):
        which = [step * step_size + u for u in range(step_size)]
        both = [
            [[in_ref[slots[pair][i], pair_of(2 * k), :] for pair in range(2)] for i in range(ROW_TILES)]
            for k in which
        ]
        for u, k in enumerate(which):
            for i in range(ROW_TILES):
                out_ref[k, :, 128 * i : 128 * (i + 1)] = jnp.concatenate(both[u][i], axis=0)
        return carry

    lax.fori_loop(0, out_ref.shape[0] // step_size, several, 0)


def per_device(spectrum, sea_mask, quad_bins, coupling, growth):
    comp_dev, width, height = spectrum.shape
    groups, tiles = lax.axis_size("comp"), lax.axis_size("tile")
    mine = lax.axis_index("comp")
    count = comp_dev * groups
    group_rows = rows_of(comp_dev)
    table = lax.dynamic_slice(jnp.asarray(courant_table().reshape(-1)), (3 * mine * comp_dev,), (3 * comp_dev,))
    tile = lax.axis_index("tile")
    odd = mine % 2 == 1
    place = jnp.stack([mine * 4 // groups, mine % 2, tile == 0, tile == tiles - 1]).astype(jnp.int32)

    smem = pl.BlockSpec(memory_space=pltpu.SMEM)
    vmem = pl.BlockSpec(memory_space=pltpu.VMEM)
    params = pltpu.CompilerParams(vmem_limit_bytes=VMEM_LIMIT)

    starts = [sum(CHUNKS[:i]) for i in range(len(CHUNKS))]
    mask = sea_mask.astype(jnp.float32)[None]
    owns = [
        jnp.concatenate([lax.slice_in_dim(spectrum, s, s + n, axis=0), mask], axis=0) for s, n in zip(starts, CHUNKS)
    ]
    half = width // 2
    halos = []
    for own in owns:
        start, end = own[:, :half], own[:, width - half :]
        one = lax.ppermute(jnp.where(odd, start, end), ("comp", "tile"), halo_pairs(groups, tiles, False))
        other = lax.ppermute(jnp.where(odd, end, start), ("comp", "tile"), halo_pairs(groups, tiles, True))
        halos.append((one, other))
    windows = window_groups(groups, tiles)

    spare = group_rows // 2 - comp_dev
    own_rows = np.arange(groups)[:, None] * group_rows + 2 * (comp_dev + np.arange(spare))[None]
    where = 2 * quad_bins.T + (group_rows - 2 * comp_dev) * (quad_bins.T // comp_dev)
    fill = jnp.asarray(np.repeat(own_rows[:, :, None], 4, axis=2).astype(np.int32))
    where = jnp.concatenate([where.reshape(groups, comp_dev, 4), fill], axis=1).reshape(-1)
    pad = lambda v: jnp.pad(v.reshape(groups, comp_dev), ((0, 0), (0, spare))).reshape(-1)
    strength, kept = pad(time_step * coupling), pad(1.0 + time_step * growth)

    moved = []
    for i, (start, size) in enumerate(zip(starts, CHUNKS)):
        moved = [
            pl.pallas_call(
                functools.partial(propagate_kernel, start),
                in_specs=[smem, smem] + [vmem] * (3 + len(moved)),
                out_specs=vmem,
                out_shape=jax.ShapeDtypeStruct((groups, rows_of(start + size), 128), jnp.float32),
                compiler_params=params,
                cost_estimate=pl.CostEstimate(flops=COST * size, bytes_accessed=16384 * size, transcendentals=0),
                name=f"propagate_{i}",
            )(place, table, owns[i], *halos[i], *moved)
        ]
    energy = lax.all_to_all(
        moved[0], ("comp", "tile"), split_axis=0, concat_axis=0, tiled=True, axis_index_groups=windows
    )

    total_rows = groups * group_rows
    fresh = pl.pallas_call(
        settle_kernel,
        in_specs=[smem, smem, smem, vmem],
        out_specs=vmem,
        out_shape=jax.ShapeDtypeStruct((total_rows, 128), jnp.float32),
        scratch_shapes=[pltpu.VMEM((total_rows, 128), jnp.float32)] * 4,
        compiler_params=params,
        name="settle",
    )(where, strength, kept, energy.reshape(total_rows, 128))

    back = lax.all_to_all(fresh.reshape(groups, group_rows, 128), "comp", split_axis=0, concat_axis=0, tiled=True)
    return pl.pallas_call(
        unpack_kernel,
        in_specs=[vmem],
        out_specs=vmem,
        out_shape=jax.ShapeDtypeStruct((comp_dev, width, height), jnp.float32),
        compiler_params=params,
        name="unpack",
    )(back)


def solution(mesh):
    return jax.shard_map(
        per_device,
        mesh=mesh,
        in_specs=(P("comp", "tile", None), P("tile", None), P(), P(), P()),
        out_specs=P("comp", "tile", None),
        check_vma=False,
    )
```

```python
import functools
import math

import jax
import jax.numpy as jnp
import numpy as np
from jax import lax
from jax.experimental import pallas as pl
from jax.experimental.pallas import tpu as pltpu
from jax.sharding import PartitionSpec as P

NDIR = 36
NFREQ = 36
SUB = 4

w_plus = 0.4096
w_minus = 3.1605
w_cross = 1.2945
time_step = 0.5

ROW_TILES = 4
SENDS = ((60, 36), (66,))
CHUNKS = tuple(sum(sizes) for sizes in SENDS)
TOGETHER = 28
VMEM_LIMIT = 40 << 20


def courant_table():
    d = np.repeat(np.arange(NDIR), NFREQ)
    level = np.tile(np.arange(NFREQ), NDIR)
    angle = 2.0 * math.pi * d / NDIR
    size = 0.7 * 0.93**level
    cos = np.where(d % (NDIR // 2) == NDIR // 4, 0.0, np.cos(angle))
    sin = np.where(d % (NDIR // 2) == 0, 0.0, np.sin(angle))
    along_x, along_y = np.abs(size * cos), np.abs(size * sin)
    return np.stack([1.0 - along_x - along_y, along_x, along_y], axis=1).astype(np.float32)


def upwind_pairs(groups, tiles):
    pairs = []
    for c in range(groups):
        east = c * 4 // groups in (0, 3)
        for t in range(tiles):
            to = t + 1 if east else t - 1
            if 0 <= to < tiles:
                pairs.append((c * tiles + t, c * tiles + to))
    return pairs


def rows_of(size):
    return -(-2 * size // 8) * 8


def pair_of(row):
    return pl.ds(pl.multiple_of(row, 2), 2)


def propagate_kernel(first, done, quarter_ref, coef_ref, own_ref, halo_ref, *refs):
    *before_refs, out_ref = refs
    size = own_ref.shape[0] - 1
    side_by_side = max(n for n in range(1, TOGETHER + 1) if size % n == 0)
    quarter = quarter_ref[0]
    lane = lax.broadcasted_iota(jnp.int32, (8, 128), 1)
    extra = out_ref.shape[1] - 2 * (done + size)
    for piece in range(out_ref.shape[0]):
        for ref in before_refs:
            out_ref[piece, : 2 * done, :] = ref[piece]
        if extra:
            out_ref[piece, 2 * (done + size) :, :] = jnp.zeros((extra, 128), jnp.float32)

    def run(east, north):
        def rows(own, halo):
            whole = jnp.concatenate([halo, own] if east else [own, halo], axis=0)
            return [whole[:, 128 * i : 128 * (i + 1)] for i in range(ROW_TILES)]

        mask = rows(own_ref[size], halo_ref[size])
        edge = lane == (0 if north else 127)
        base = 4 if east else 0

        def several(step, carry):
            which = [step * side_by_side + u for u in range(side_by_side)]
            coefs = [[coef_ref[3 * (first + k) + i] for i in range(3)] for k in which]
            fields = [rows(own_ref[k], halo_ref[k]) for k in which]
            for _ in range(SUB):
                turned = [[pltpu.roll(v, 1 if north else 127, 1) for v in field] for field in fields]
                cols = [[pltpu.roll(v, 1 if east else 7, 0) for v in field] for field in fields]
                fresh = []
                for u, (stay, side, along) in enumerate(coefs):
                    field = []
                    for i in range(ROW_TILES):
                        j = i - 1 if north else i + 1
                        over = turned[u][j] if 0 <= j < ROW_TILES else 0.0
                        upwind_row = jnp.where(edge, over, turned[u][i])
                        field.append(mask[i] * (stay * fields[u][i] + side * cols[u][i] + along * upwind_row))
                    fresh.append(field)
                fields = fresh
            for u, k in enumerate(which):
                for i, v in enumerate(fields[u]):
                    for pair in range(2):
                        at = base + 2 * pair
                        out_ref[pair * ROW_TILES + i, pair_of(2 * (done + k)), :] = v[at : at + 2, :]
            return carry

        lax.fori_loop(0, size // side_by_side, several, 0)

    for value, (east, north) in enumerate(((True, True), (False, True), (False, False), (True, False))):
        pl.when(quarter == value)(functools.partial(run, east, north))


def settle_kernel(bins_ref, strength_ref, kept_ref, *refs):
    pieces = refs[: len(CHUNKS)]
    out_ref, energy_ref, *parts = refs[len(CHUNKS) :]
    total_rows = energy_ref.shape[0]
    groups = pieces[0].shape[0]

    def tile_of(t):
        return pl.ds(pl.multiple_of(8 * t, 8), 8)

    def take(piece, shift, g, carry):
        for t in range(piece.shape[1] // 8):
            here = pl.ds(pl.multiple_of(g * (total_rows // groups) + shift + 8 * t, 8), 8)
            energy_ref[here, :] = piece[g, 8 * t : 8 * t + 8, :]
            for ref in parts:
                ref[here, :] = jnp.zeros((8, 128), jnp.float32)
        return carry

    shift = 0
    for piece in pieces:
        lax.fori_loop(0, groups, functools.partial(take, piece, shift), 0)
        shift += piece.shape[1]

    def one(k, carry):
        rows = [pair_of(bins_ref[4 * k + j]) for j in range(4)]
        here = pair_of(2 * k)
        energy = energy_ref[here, :]
        scaled = strength_ref[k] * energy
        cross, squared = (2.0 * w_cross) * scaled, scaled * energy
        squared_plus, squared_minus = w_plus * squared, w_minus * squared
        deltas = []
        for mirror in range(2):
            plus, minus = (energy_ref[row, :] for row in rows[2 * mirror : 2 * mirror + 2])
            deltas.append(minus * (squared_minus - cross * plus) + squared_plus * plus)
        for j, row in enumerate(rows):
            parts[j][row, :] = parts[j][row, :] + deltas[j // 2]
        out_ref[here, :] = kept_ref[k] * energy - 2.0 * (deltas[0] + deltas[1])
        return carry

    lax.fori_loop(0, total_rows // 2, one, 0, unroll=16)

    def gather(t, carry):
        s = tile_of(t)
        a, b, c, d = (ref[s, :] for ref in parts)
        out_ref[s, :] = out_ref[s, :] + ((a + b) + (c + d))
        return carry

    lax.fori_loop(0, total_rows // 8, gather, 0, unroll=8)


def unpack_kernel(in_ref, out_ref):
    step_size = 9

    def several(step, carry):
        which = [step * step_size + u for u in range(step_size)]
        both = [
            [[in_ref[pair * ROW_TILES + i, pair_of(2 * k), :] for pair in range(2)] for i in range(ROW_TILES)]
            for k in which
        ]
        for u, k in enumerate(which):
            for i in range(ROW_TILES):
                out_ref[k, :, 128 * i : 128 * (i + 1)] = jnp.concatenate(both[u][i], axis=0)
        return carry

    lax.fori_loop(0, out_ref.shape[0] // step_size, several, 0)


def per_device(spectrum, sea_mask, quad_bins, coupling, growth):
    comp_dev, width, height = spectrum.shape
    groups, tiles = lax.axis_size("comp"), lax.axis_size("tile")
    mine = lax.axis_index("comp")
    count = comp_dev * groups
    group_rows = sum(rows_of(size) for size in CHUNKS)
    pairs = upwind_pairs(groups, tiles)
    table = lax.dynamic_slice(jnp.asarray(courant_table().reshape(-1)), (3 * mine * comp_dev,), (3 * comp_dev,))
    quarter = (mine * 4 // groups).reshape(1).astype(jnp.int32)

    smem = pl.BlockSpec(memory_space=pltpu.SMEM)
    vmem = pl.BlockSpec(memory_space=pltpu.VMEM)
    params = pltpu.CompilerParams(vmem_limit_bytes=VMEM_LIMIT)

    sizes = sum(SENDS, ())
    starts = [sum(sizes[:i]) for i in range(len(sizes))]
    mask = sea_mask.astype(jnp.float32)[None]
    owns = [
        jnp.concatenate([lax.slice_in_dim(spectrum, s, s + n, axis=0), mask], axis=0) for s, n in zip(starts, sizes)
    ]
    halos = [lax.ppermute(own, ("comp", "tile"), pairs) for own in owns]

    spare = group_rows // 2 - comp_dev
    own_rows = np.arange(groups)[:, None] * group_rows + 2 * (comp_dev + np.arange(spare))[None]
    where = 2 * quad_bins.T + (group_rows - 2 * comp_dev) * (quad_bins.T // comp_dev)
    fill = jnp.asarray(np.repeat(own_rows[:, :, None], 4, axis=2).astype(np.int32))
    where = jnp.concatenate([where.reshape(groups, comp_dev, 4), fill], axis=1).reshape(-1)

    pad = lambda v: jnp.pad(v.reshape(groups, comp_dev), ((0, 0), (0, spare))).reshape(-1)
    strength, kept = pad(time_step * coupling), pad(1.0 + time_step * growth)

    pieces = []
    i = 0
    for together in SENDS:
        moved, done = [], 0
        for size in together:
            moved = [
                pl.pallas_call(
                    functools.partial(propagate_kernel, starts[i], done),
                    in_specs=[smem, smem] + [vmem] * (2 + len(moved)),
                    out_specs=vmem,
                    out_shape=jax.ShapeDtypeStruct((groups, rows_of(done + size), 128), jnp.float32),
                    compiler_params=params,
                    cost_estimate=pl.CostEstimate(
                        flops=200_000 * size, bytes_accessed=24_000 * size, transcendentals=0
                    ),
                    name=f"propagate_{i}",
                )(quarter, table, owns[i], halos[i], *moved)
            ]
            done += size
            i += 1
        pieces.append(lax.all_to_all(moved[0], "comp", split_axis=0, concat_axis=0, tiled=True))

    total_rows = groups * group_rows
    fresh = pl.pallas_call(
        settle_kernel,
        in_specs=[smem, smem, smem] + [vmem] * len(CHUNKS),
        out_specs=vmem,
        out_shape=jax.ShapeDtypeStruct((total_rows, 128), jnp.float32),
        scratch_shapes=[pltpu.VMEM((total_rows, 128), jnp.float32)] * 5,
        compiler_params=params,
        name="settle",
    )(where, strength, kept, *pieces)

    back = lax.all_to_all(fresh.reshape(groups, group_rows, 128), "comp", split_axis=0, concat_axis=0, tiled=True)
    return pl.pallas_call(
        unpack_kernel,
        in_specs=[vmem],
        out_specs=vmem,
        out_shape=jax.ShapeDtypeStruct((comp_dev, width, height), jnp.float32),
        compiler_params=params,
        name="unpack",
    )(back)


def solution(mesh):
    return jax.shard_map(
        per_device,
        mesh=mesh,
        in_specs=(P("comp", "tile", None), P("tile", None), P(), P(), P()),
        out_specs=P("comp", "tile", None),
        check_vma=False,
    )
```

```python
import functools
import math

import jax
import jax.numpy as jnp
import numpy as np
from jax import lax
from jax.experimental import pallas as pl
from jax.experimental.pallas import tpu as pltpu
from jax.sharding import PartitionSpec as P

NDIR = 36
NFREQ = 36
SUB = 4

w_plus = 0.4096
w_minus = 3.1605
w_cross = 1.2945
time_step = 0.5

ROW_TILES = 4
CHUNKS = (96, 66)
TOGETHER = 28
VMEM_LIMIT = 40 << 20


def courant_table():
    d = np.repeat(np.arange(NDIR), NFREQ)
    level = np.tile(np.arange(NFREQ), NDIR)
    angle = 2.0 * math.pi * d / NDIR
    size = 0.7 * 0.93**level
    cos = np.where(d % (NDIR // 2) == NDIR // 4, 0.0, np.cos(angle))
    sin = np.where(d % (NDIR // 2) == 0, 0.0, np.sin(angle))
    along_x, along_y = np.abs(size * cos), np.abs(size * sin)
    return np.stack([1.0 - along_x - along_y, along_x, along_y], axis=1).astype(np.float32)


def upwind_pairs(groups, tiles):
    pairs = []
    for c in range(groups):
        east = c * 4 // groups in (0, 3)
        for t in range(tiles):
            to = t + 1 if east else t - 1
            if 0 <= to < tiles:
                pairs.append((c * tiles + t, c * tiles + to))
    return pairs


def rows_of(size):
    return -(-2 * size // 8) * 8


def pair_of(row):
    return pl.ds(pl.multiple_of(row, 2), 2)


def pack_kernel(start, spectrum_ref, mask_ref, out_ref, sem):
    size = out_ref.shape[0] - 1
    copy = pltpu.make_async_copy(spectrum_ref.at[pl.ds(start, size)], out_ref.at[pl.ds(0, size)], sem)
    copy.start()
    out_ref[size] = mask_ref[...].astype(jnp.float32)
    copy.wait()


def propagate_kernel(first, quarter_ref, coef_ref, own_ref, halo_ref, out_ref):
    size = own_ref.shape[0] - 1
    side_by_side = max(n for n in range(1, TOGETHER + 1) if size % n == 0)
    quarter = quarter_ref[0]
    lane = lax.broadcasted_iota(jnp.int32, (8, 128), 1)
    extra = out_ref.shape[1] - 2 * size
    if extra:
        for piece in range(out_ref.shape[0]):
            out_ref[piece, 2 * size :, :] = jnp.zeros((extra, 128), jnp.float32)

    def run(east, north):
        def rows(own, halo):
            whole = jnp.concatenate([halo, own] if east else [own, halo], axis=0)
            return [whole[:, 128 * i : 128 * (i + 1)] for i in range(ROW_TILES)]

        mask = rows(own_ref[size], halo_ref[size])
        edge = lane == (0 if north else 127)
        base = 4 if east else 0

        def several(step, carry):
            which = [step * side_by_side + u for u in range(side_by_side)]
            coefs = [[coef_ref[3 * (first + k) + i] for i in range(3)] for k in which]
            fields = [rows(own_ref[k], halo_ref[k]) for k in which]
            for _ in range(SUB):
                turned = [[pltpu.roll(v, 1 if north else 127, 1) for v in field] for field in fields]
                cols = [[pltpu.roll(v, 1 if east else 7, 0) for v in field] for field in fields]
                fresh = []
                for u, (stay, side, along) in enumerate(coefs):
                    field = []
                    for i in range(ROW_TILES):
                        j = i - 1 if north else i + 1
                        over = turned[u][j] if 0 <= j < ROW_TILES else 0.0
                        upwind_row = jnp.where(edge, over, turned[u][i])
                        field.append(mask[i] * (stay * fields[u][i] + side * cols[u][i] + along * upwind_row))
                    fresh.append(field)
                fields = fresh
            for u, k in enumerate(which):
                for i, v in enumerate(fields[u]):
                    for pair in range(2):
                        at = base + 2 * pair
                        out_ref[pair * ROW_TILES + i, pair_of(2 * k), :] = v[at : at + 2, :]
            return carry

        lax.fori_loop(0, size // side_by_side, several, 0)

    for value, (east, north) in enumerate(((True, True), (False, True), (False, False), (True, False))):
        pl.when(quarter == value)(functools.partial(run, east, north))


def settle_kernel(bins_ref, strength_ref, kept_ref, *refs):
    pieces = refs[: len(CHUNKS)]
    out_ref, energy_ref, *parts = refs[len(CHUNKS) :]
    total_rows = energy_ref.shape[0]
    groups = pieces[0].shape[0]

    def tile_of(t):
        return pl.ds(pl.multiple_of(8 * t, 8), 8)

    def take(piece, shift, g, carry):
        for t in range(piece.shape[1] // 8):
            here = pl.ds(pl.multiple_of(g * (total_rows // groups) + shift + 8 * t, 8), 8)
            energy_ref[here, :] = piece[g, 8 * t : 8 * t + 8, :]
            for ref in parts:
                ref[here, :] = jnp.zeros((8, 128), jnp.float32)
        return carry

    shift = 0
    for piece in pieces:
        lax.fori_loop(0, groups, functools.partial(take, piece, shift), 0)
        shift += piece.shape[1]

    def one(k, carry):
        rows = [pair_of(bins_ref[4 * k + j]) for j in range(4)]
        here = pair_of(2 * k)
        energy = energy_ref[here, :]
        scaled = strength_ref[k] * energy
        cross, squared = (2.0 * w_cross) * scaled, scaled * energy
        squared_plus, squared_minus = w_plus * squared, w_minus * squared
        deltas = []
        for mirror in range(2):
            plus, minus = (energy_ref[row, :] for row in rows[2 * mirror : 2 * mirror + 2])
            deltas.append(minus * (squared_minus - cross * plus) + squared_plus * plus)
        for j, row in enumerate(rows):
            parts[j][row, :] = parts[j][row, :] + deltas[j // 2]
        out_ref[here, :] = kept_ref[k] * energy - 2.0 * (deltas[0] + deltas[1])
        return carry

    lax.fori_loop(0, total_rows // 2, one, 0, unroll=32)

    def gather(t, carry):
        s = tile_of(t)
        a, b, c, d = (ref[s, :] for ref in parts)
        out_ref[s, :] = out_ref[s, :] + ((a + b) + (c + d))
        return carry

    lax.fori_loop(0, total_rows // 8, gather, 0, unroll=8)


def unpack_kernel(in_ref, out_ref):
    size, together = out_ref.shape[0], 9
    first = pl.program_id(0) * size

    def several(step, carry):
        which = [step * together + u for u in range(together)]
        both = [
            [
                [in_ref[pair * ROW_TILES + i, pair_of(2 * (first + k)), :] for pair in range(2)]
                for i in range(ROW_TILES)
            ]
            for k in which
        ]
        for u, k in enumerate(which):
            for i in range(ROW_TILES):
                out_ref[k, :, 128 * i : 128 * (i + 1)] = jnp.concatenate(both[u][i], axis=0)
        return carry

    lax.fori_loop(0, size // together, several, 0)


def per_device(spectrum, sea_mask, quad_bins, coupling, growth):
    comp_dev, width, height = spectrum.shape
    groups, tiles = lax.axis_size("comp"), lax.axis_size("tile")
    mine = lax.axis_index("comp")
    count = comp_dev * groups
    group_rows = sum(rows_of(size) for size in CHUNKS)
    pairs = upwind_pairs(groups, tiles)
    table = lax.dynamic_slice(jnp.asarray(courant_table().reshape(-1)), (3 * mine * comp_dev,), (3 * comp_dev,))
    quarter = (mine * 4 // groups).reshape(1).astype(jnp.int32)

    smem = pl.BlockSpec(memory_space=pltpu.SMEM)
    vmem = pl.BlockSpec(memory_space=pltpu.VMEM)
    params = pltpu.CompilerParams(vmem_limit_bytes=VMEM_LIMIT)

    starts = [sum(CHUNKS[:i]) for i in range(len(CHUNKS))]
    owns = [
        pl.pallas_call(
            functools.partial(pack_kernel, start),
            in_specs=[pl.BlockSpec(memory_space=pl.ANY), vmem],
            out_specs=vmem,
            out_shape=jax.ShapeDtypeStruct((size + 1, width, height), jnp.float32),
            scratch_shapes=[pltpu.SemaphoreType.DMA],
            name=f"pack_{i}",
        )(spectrum, sea_mask)
        for i, (start, size) in enumerate(zip(starts, CHUNKS))
    ]
    halos = [lax.ppermute(own, ("comp", "tile"), pairs) for own in owns]

    spare = group_rows // 2 - comp_dev
    own_rows = np.arange(groups)[:, None] * group_rows + 2 * (comp_dev + np.arange(spare))[None]
    where = 2 * quad_bins.T + (group_rows - 2 * comp_dev) * (quad_bins.T // comp_dev)
    fill = jnp.asarray(np.repeat(own_rows[:, :, None], 4, axis=2).astype(np.int32))
    where = jnp.concatenate([where.reshape(groups, comp_dev, 4), fill], axis=1).reshape(-1)

    pad = lambda v: jnp.pad(v.reshape(groups, comp_dev), ((0, 0), (0, spare))).reshape(-1)
    strength, kept = pad(time_step * coupling), pad(1.0 + time_step * growth)

    pieces = []
    for i, (start, size) in enumerate(zip(starts, CHUNKS)):
        moved = pl.pallas_call(
            functools.partial(propagate_kernel, start),
            in_specs=[smem, smem, vmem, vmem],
            out_specs=vmem,
            out_shape=jax.ShapeDtypeStruct((groups, rows_of(size), 128), jnp.float32),
            compiler_params=params,
            cost_estimate=pl.CostEstimate(flops=100 * size * 2048, bytes_accessed=12 * size * 2048, transcendentals=0),
            name=f"propagate_{i}",
        )(quarter, table, owns[i], halos[i])
        pieces.append(lax.all_to_all(moved, "comp", split_axis=0, concat_axis=0, tiled=True))

    total_rows = groups * group_rows
    fresh = pl.pallas_call(
        settle_kernel,
        in_specs=[smem, smem, smem] + [vmem] * len(CHUNKS),
        out_specs=vmem,
        out_shape=jax.ShapeDtypeStruct((total_rows, 128), jnp.float32),
        scratch_shapes=[pltpu.VMEM((total_rows, 128), jnp.float32)] * 5,
        compiler_params=params,
        name="settle",
    )(where, strength, kept, *pieces)

    back = lax.all_to_all(fresh.reshape(groups, group_rows, 128), "comp", split_axis=0, concat_axis=0, tiled=True)
    return pl.pallas_call(
        unpack_kernel,
        grid=(2,),
        in_specs=[vmem],
        out_specs=pl.BlockSpec((comp_dev // 2, width, height), lambda i: (i, 0, 0)),
        out_shape=jax.ShapeDtypeStruct((comp_dev, width, height), jnp.float32),
        compiler_params=params,
        name="unpack",
    )(back)


def solution(mesh):
    return jax.shard_map(
        per_device,
        mesh=mesh,
        in_specs=(P("comp", "tile", None), P("tile", None), P(), P(), P()),
        out_specs=P("comp", "tile", None),
        check_vma=False,
    )
```

```python
import functools
import math

import jax
import jax.numpy as jnp
import numpy as np
from jax import lax
from jax.experimental import pallas as pl
from jax.experimental.pallas import tpu as pltpu
from jax.sharding import PartitionSpec as P

NDIR = 36
NFREQ = 36
SUB = 4

w_plus = 0.4096
w_minus = 3.1605
w_cross = 1.2945
time_step = 0.5

ROW_TILES = 4
CHUNKS = (92, 70)
TOGETHER = 35
VMEM_LIMIT = 40 << 20


def courant_table():
    d = np.repeat(np.arange(NDIR), NFREQ)
    level = np.tile(np.arange(NFREQ), NDIR)
    angle = 2.0 * math.pi * d / NDIR
    size = 0.7 * 0.93**level
    cos = np.where(d % (NDIR // 2) == NDIR // 4, 0.0, np.cos(angle))
    sin = np.where(d % (NDIR // 2) == 0, 0.0, np.sin(angle))
    along_x, along_y = np.abs(size * cos), np.abs(size * sin)
    return np.stack([1.0 - along_x - along_y, along_x, along_y], axis=1).astype(np.float32)


def upwind_pairs(groups, tiles):
    pairs = []
    for c in range(groups):
        east = c * 4 // groups in (0, 3)
        for t in range(tiles):
            to = t + 1 if east else t - 1
            if 0 <= to < tiles:
                pairs.append((c * tiles + t, c * tiles + to))
    return pairs


def rows_of(size):
    return -(-2 * size // 8) * 8


def pair_of(row):
    return pl.ds(pl.multiple_of(row, 2), 2)


def propagate_kernel(first, quarter_ref, coef_ref, own_ref, halo_ref, out_ref):
    size = own_ref.shape[0] - 1
    side_by_side = max(n for n in range(1, TOGETHER + 1) if size % n == 0)
    quarter = quarter_ref[0]
    lane = lax.broadcasted_iota(jnp.int32, (8, 128), 1)
    extra = out_ref.shape[1] - 2 * size
    if extra:
        for piece in range(out_ref.shape[0]):
            out_ref[piece, 2 * size :, :] = jnp.zeros((extra, 128), jnp.float32)

    def run(east, north):
        def rows(own, halo):
            whole = jnp.concatenate([halo, own] if east else [own, halo], axis=0)
            return [whole[:, 128 * i : 128 * (i + 1)] for i in range(ROW_TILES)]

        mask = rows(own_ref[size], halo_ref[size])
        edge = lane == (0 if north else 127)
        base = 4 if east else 0

        def several(step, carry):
            which = [step * side_by_side + u for u in range(side_by_side)]
            coefs = [[coef_ref[3 * (first + k) + i] for i in range(3)] for k in which]
            fields = [rows(own_ref[k], halo_ref[k]) for k in which]
            for _ in range(SUB):
                turned = [[pltpu.roll(v, 1 if north else 127, 1) for v in field] for field in fields]
                cols = [[pltpu.roll(v, 1 if east else 7, 0) for v in field] for field in fields]
                fresh = []
                for u, (stay, side, along) in enumerate(coefs):
                    field = []
                    for i in range(ROW_TILES):
                        j = i - 1 if north else i + 1
                        over = turned[u][j] if 0 <= j < ROW_TILES else 0.0
                        upwind_row = jnp.where(edge, over, turned[u][i])
                        field.append(mask[i] * (stay * fields[u][i] + side * cols[u][i] + along * upwind_row))
                    fresh.append(field)
                fields = fresh
            for u, k in enumerate(which):
                for i, v in enumerate(fields[u]):
                    for pair in range(2):
                        at = base + 2 * pair
                        out_ref[pair * ROW_TILES + i, pair_of(2 * k), :] = v[at : at + 2, :]
            return carry

        lax.fori_loop(0, size // side_by_side, several, 0)

    for value, (east, north) in enumerate(((True, True), (False, True), (False, False), (True, False))):
        pl.when(quarter == value)(functools.partial(run, east, north))


def settle_kernel(bins_ref, strength_ref, kept_ref, *refs):
    pieces = refs[: len(CHUNKS)]
    out_ref, energy_ref, *parts = refs[len(CHUNKS) :]
    total_rows = energy_ref.shape[0]
    groups = pieces[0].shape[0]

    def tile_of(t):
        return pl.ds(pl.multiple_of(8 * t, 8), 8)

    def take(piece, shift, g, carry):
        for t in range(piece.shape[1] // 8):
            here = pl.ds(pl.multiple_of(g * (total_rows // groups) + shift + 8 * t, 8), 8)
            energy_ref[here, :] = piece[g, 8 * t : 8 * t + 8, :]
            for ref in parts:
                ref[here, :] = jnp.zeros((8, 128), jnp.float32)
        return carry

    shift = 0
    for piece in pieces:
        lax.fori_loop(0, groups, functools.partial(take, piece, shift), 0)
        shift += piece.shape[1]

    def one(k, carry):
        rows = [pair_of(bins_ref[4 * k + j]) for j in range(4)]
        here = pair_of(2 * k)
        energy = energy_ref[here, :]
        scaled = strength_ref[k] * energy
        cross, squared = (2.0 * w_cross) * scaled, scaled * energy
        squared_plus, squared_minus = w_plus * squared, w_minus * squared
        deltas = []
        for mirror in range(2):
            plus, minus = (energy_ref[row, :] for row in rows[2 * mirror : 2 * mirror + 2])
            deltas.append(minus * (squared_minus - cross * plus) + squared_plus * plus)
        for j, row in enumerate(rows):
            parts[j][row, :] = parts[j][row, :] + deltas[j // 2]
        out_ref[here, :] = kept_ref[k] * energy - 2.0 * (deltas[0] + deltas[1])
        return carry

    lax.fori_loop(0, total_rows // 2, one, 0, unroll=32)

    def gather(t, carry):
        s = tile_of(t)
        a, b, c, d = (ref[s, :] for ref in parts)
        out_ref[s, :] = out_ref[s, :] + ((a + b) + (c + d))
        return carry

    lax.fori_loop(0, total_rows // 8, gather, 0, unroll=8)


def unpack_kernel(in_ref, out_ref):
    size, together = out_ref.shape[0], 9
    first = pl.program_id(0) * size

    def several(step, carry):
        which = [step * together + u for u in range(together)]
        both = [
            [
                [in_ref[pair * ROW_TILES + i, pair_of(2 * (first + k)), :] for pair in range(2)]
                for i in range(ROW_TILES)
            ]
            for k in which
        ]
        for u, k in enumerate(which):
            for i in range(ROW_TILES):
                out_ref[k, :, 128 * i : 128 * (i + 1)] = jnp.concatenate(both[u][i], axis=0)
        return carry

    lax.fori_loop(0, size // together, several, 0)


def per_device(spectrum, sea_mask, quad_bins, coupling, growth):
    comp_dev, width, height = spectrum.shape
    groups, tiles = lax.axis_size("comp"), lax.axis_size("tile")
    mine = lax.axis_index("comp")
    count = comp_dev * groups
    group_rows = sum(rows_of(size) for size in CHUNKS)
    pairs = upwind_pairs(groups, tiles)
    table = lax.dynamic_slice(jnp.asarray(courant_table().reshape(-1)), (3 * mine * comp_dev,), (3 * comp_dev,))
    quarter = (mine * 4 // groups).reshape(1).astype(jnp.int32)

    smem = pl.BlockSpec(memory_space=pltpu.SMEM)
    vmem = pl.BlockSpec(memory_space=pltpu.VMEM)
    params = pltpu.CompilerParams(vmem_limit_bytes=VMEM_LIMIT)

    starts = [sum(CHUNKS[:i]) for i in range(len(CHUNKS))]
    mask = sea_mask.astype(jnp.float32)[None]
    owns = [
        jnp.concatenate([lax.slice_in_dim(spectrum, s, s + n, axis=0), mask], axis=0) for s, n in zip(starts, CHUNKS)
    ]
    halos = [lax.ppermute(own, ("comp", "tile"), pairs) for own in owns]

    spare = group_rows // 2 - comp_dev
    own_rows = np.arange(groups)[:, None] * group_rows + 2 * (comp_dev + np.arange(spare))[None]
    where = 2 * quad_bins.T + (group_rows - 2 * comp_dev) * (quad_bins.T // comp_dev)
    fill = jnp.asarray(np.repeat(own_rows[:, :, None], 4, axis=2).astype(np.int32))
    where = jnp.concatenate([where.reshape(groups, comp_dev, 4), fill], axis=1).reshape(-1)

    pad = lambda v: jnp.pad(v.reshape(groups, comp_dev), ((0, 0), (0, spare))).reshape(-1)
    strength, kept = pad(time_step * coupling), pad(1.0 + time_step * growth)

    pieces = []
    for i, (start, size) in enumerate(zip(starts, CHUNKS)):
        moved = pl.pallas_call(
            functools.partial(propagate_kernel, start),
            in_specs=[smem, smem, vmem, vmem],
            out_specs=vmem,
            out_shape=jax.ShapeDtypeStruct((groups, rows_of(size), 128), jnp.float32),
            compiler_params=params,
            cost_estimate=pl.CostEstimate(flops=100 * size * 2048, bytes_accessed=12 * size * 2048, transcendentals=0),
            name=f"propagate_{i}",
        )(quarter, table, owns[i], halos[i])
        pieces.append(lax.all_to_all(moved, "comp", split_axis=0, concat_axis=0, tiled=True))

    total_rows = groups * group_rows
    fresh = pl.pallas_call(
        settle_kernel,
        in_specs=[smem, smem, smem] + [vmem] * len(CHUNKS),
        out_specs=vmem,
        out_shape=jax.ShapeDtypeStruct((total_rows, 128), jnp.float32),
        scratch_shapes=[pltpu.VMEM((total_rows, 128), jnp.float32)] * 5,
        compiler_params=params,
        name="settle",
    )(where, strength, kept, *pieces)

    back = lax.all_to_all(fresh.reshape(groups, group_rows, 128), "comp", split_axis=0, concat_axis=0, tiled=True)
    return pl.pallas_call(
        unpack_kernel,
        grid=(2,),
        in_specs=[vmem],
        out_specs=pl.BlockSpec((comp_dev // 2, width, height), lambda i: (i, 0, 0)),
        out_shape=jax.ShapeDtypeStruct((comp_dev, width, height), jnp.float32),
        compiler_params=params,
        name="unpack",
    )(back)


def solution(mesh):
    return jax.shard_map(
        per_device,
        mesh=mesh,
        in_specs=(P("comp", "tile", None), P("tile", None), P(), P(), P()),
        out_specs=P("comp", "tile", None),
        check_vma=False,
    )
```

```python
import functools
import math

import jax
import jax.numpy as jnp
import numpy as np
from jax import lax
from jax.experimental import pallas as pl
from jax.experimental.pallas import tpu as pltpu
from jax.sharding import PartitionSpec as P

NDIR = 36
NFREQ = 36
SUB = 4

w_plus = 0.4096
w_minus = 3.1605
w_cross = 1.2945
time_step = 0.5

ROW_TILES = 4
CHUNKS = (84, 78)
TOGETHER = 35
VMEM_LIMIT = 40 << 20


def courant_table():
    d = np.repeat(np.arange(NDIR), NFREQ)
    level = np.tile(np.arange(NFREQ), NDIR)
    angle = 2.0 * math.pi * d / NDIR
    size = 0.7 * 0.93**level
    cos = np.where(d % (NDIR // 2) == NDIR // 4, 0.0, np.cos(angle))
    sin = np.where(d % (NDIR // 2) == 0, 0.0, np.sin(angle))
    along_x, along_y = np.abs(size * cos), np.abs(size * sin)
    return np.stack([1.0 - along_x - along_y, along_x, along_y], axis=1).astype(np.float32)


def upwind_pairs(groups, tiles):
    pairs = []
    for c in range(groups):
        east = c * 4 // groups in (0, 3)
        for t in range(tiles):
            to = t + 1 if east else t - 1
            if 0 <= to < tiles:
                pairs.append((c * tiles + t, c * tiles + to))
    return pairs


def rows_of(size):
    return -(-2 * size // 8) * 8


def pair_of(row):
    return pl.ds(pl.multiple_of(row, 2), 2)


def together(size):
    return max(n for n in range(1, TOGETHER + 1) if size % n == 0)


def propagate_kernel(first, quarter_ref, coef_ref, own_ref, halo_ref, target_ref, *scratch):
    out_ref, sems = scratch or (target_ref, None)
    size = own_ref.shape[0] - 1
    side_by_side = together(size)
    quarter = quarter_ref[0]
    lane = lax.broadcasted_iota(jnp.int32, (8, 128), 1)
    extra = out_ref.shape[1] - 2 * size
    if extra:
        for piece in range(out_ref.shape[0]):
            out_ref[piece, 2 * size :, :] = jnp.zeros((extra, 128), jnp.float32)

    def run(east, north):
        def rows(own, halo):
            whole = jnp.concatenate([halo, own] if east else [own, halo], axis=0)
            return [whole[:, 128 * i : 128 * (i + 1)] for i in range(ROW_TILES)]

        mask = rows(own_ref[size], halo_ref[size])
        edge = lane == (0 if north else 127)
        base = 4 if east else 0

        def several(step, carry):
            which = [step * side_by_side + u for u in range(side_by_side)]
            coefs = [[coef_ref[3 * (first + k) + i] for i in range(3)] for k in which]
            fields = [rows(own_ref[k], halo_ref[k]) for k in which]
            for _ in range(SUB):
                turned = [[pltpu.roll(v, 1 if north else 127, 1) for v in field] for field in fields]
                cols = [[pltpu.roll(v, 1 if east else 7, 0) for v in field] for field in fields]
                fresh = []
                for u, (stay, side, along) in enumerate(coefs):
                    field = []
                    for i in range(ROW_TILES):
                        j = i - 1 if north else i + 1
                        over = turned[u][j] if 0 <= j < ROW_TILES else 0.0
                        upwind_row = jnp.where(edge, over, turned[u][i])
                        field.append(mask[i] * (stay * fields[u][i] + side * cols[u][i] + along * upwind_row))
                    fresh.append(field)
                fields = fresh
            for u, k in enumerate(which):
                for i, v in enumerate(fields[u]):
                    for pair in range(2):
                        at = base + 2 * pair
                        out_ref[pair * ROW_TILES + i, pair_of(2 * k), :] = v[at : at + 2, :]
            return carry

        def leave(step):
            rows = pl.ds(pl.multiple_of(2 * side_by_side * step, 8), 2 * side_by_side)
            return pltpu.make_async_copy(out_ref.at[:, rows, :], target_ref.at[:, rows, :], sems.at[step])

        if sems is None:
            lax.fori_loop(0, size // side_by_side, several, 0)
            return
        for step in range(size // side_by_side):
            several(step, 0)
            leave(step).start()
        for step in range(size // side_by_side):
            leave(step).wait()

    for value, (east, north) in enumerate(((True, True), (False, True), (False, False), (True, False))):
        pl.when(quarter == value)(functools.partial(run, east, north))


def settle_kernel(bins_ref, strength_ref, kept_ref, *refs):
    pieces = refs[: len(CHUNKS)]
    out_ref, energy_ref, *parts = refs[len(CHUNKS) :]
    total_rows = energy_ref.shape[0]
    groups = pieces[0].shape[0]

    def tile_of(t):
        return pl.ds(pl.multiple_of(8 * t, 8), 8)

    def take(piece, shift, g, carry):
        for t in range(piece.shape[1] // 8):
            here = pl.ds(pl.multiple_of(g * (total_rows // groups) + shift + 8 * t, 8), 8)
            energy_ref[here, :] = piece[g, 8 * t : 8 * t + 8, :]
            for ref in parts:
                ref[here, :] = jnp.zeros((8, 128), jnp.float32)
        return carry

    shift = 0
    for piece in pieces:
        lax.fori_loop(0, groups, functools.partial(take, piece, shift), 0)
        shift += piece.shape[1]

    def one(k, carry):
        rows = [pair_of(bins_ref[4 * k + j]) for j in range(4)]
        here = pair_of(2 * k)
        energy = energy_ref[here, :]
        scaled = strength_ref[k] * energy
        cross, squared = (2.0 * w_cross) * scaled, scaled * energy
        squared_plus, squared_minus = w_plus * squared, w_minus * squared
        deltas = []
        for mirror in range(2):
            plus, minus = (energy_ref[row, :] for row in rows[2 * mirror : 2 * mirror + 2])
            deltas.append(minus * (squared_minus - cross * plus) + squared_plus * plus)
        for j, row in enumerate(rows):
            parts[j][row, :] = parts[j][row, :] + deltas[j // 2]
        out_ref[here, :] = kept_ref[k] * energy - 2.0 * (deltas[0] + deltas[1])
        return carry

    lax.fori_loop(0, total_rows // 2, one, 0, unroll=32)

    def gather(t, carry):
        s = tile_of(t)
        a, b, c, d = (ref[s, :] for ref in parts)
        out_ref[s, :] = out_ref[s, :] + ((a + b) + (c + d))
        return carry

    lax.fori_loop(0, total_rows // 8, gather, 0, unroll=8)


def unpack_kernel(in_ref, out_ref):
    size, several_at_once = out_ref.shape[0], 9
    first = pl.program_id(0) * size

    def several(step, carry):
        which = [step * several_at_once + u for u in range(several_at_once)]
        both = [
            [
                [in_ref[pair * ROW_TILES + i, pair_of(2 * (first + k)), :] for pair in range(2)]
                for i in range(ROW_TILES)
            ]
            for k in which
        ]
        for u, k in enumerate(which):
            for i in range(ROW_TILES):
                out_ref[k, :, 128 * i : 128 * (i + 1)] = jnp.concatenate(both[u][i], axis=0)
        return carry

    lax.fori_loop(0, size // several_at_once, several, 0)


def per_device(spectrum, sea_mask, quad_bins, coupling, growth):
    comp_dev, width, height = spectrum.shape
    groups, tiles = lax.axis_size("comp"), lax.axis_size("tile")
    mine = lax.axis_index("comp")
    count = comp_dev * groups
    group_rows = sum(rows_of(size) for size in CHUNKS)
    pairs = upwind_pairs(groups, tiles)
    table = lax.dynamic_slice(jnp.asarray(courant_table().reshape(-1)), (3 * mine * comp_dev,), (3 * comp_dev,))
    quarter = (mine * 4 // groups).reshape(1).astype(jnp.int32)

    smem = pl.BlockSpec(memory_space=pltpu.SMEM)
    vmem = pl.BlockSpec(memory_space=pltpu.VMEM)
    params = pltpu.CompilerParams(vmem_limit_bytes=VMEM_LIMIT)

    starts = [sum(CHUNKS[:i]) for i in range(len(CHUNKS))]
    mask = sea_mask.astype(jnp.float32)[None]
    owns = [
        jnp.concatenate([lax.slice_in_dim(spectrum, s, s + n, axis=0), mask], axis=0) for s, n in zip(starts, CHUNKS)
    ]
    halos = [lax.ppermute(own, ("comp", "tile"), pairs) for own in owns]

    spare = group_rows // 2 - comp_dev
    own_rows = np.arange(groups)[:, None] * group_rows + 2 * (comp_dev + np.arange(spare))[None]
    where = 2 * quad_bins.T + (group_rows - 2 * comp_dev) * (quad_bins.T // comp_dev)
    fill = jnp.asarray(np.repeat(own_rows[:, :, None], 4, axis=2).astype(np.int32))
    where = jnp.concatenate([where.reshape(groups, comp_dev, 4), fill], axis=1).reshape(-1)

    pad = lambda v: jnp.pad(v.reshape(groups, comp_dev), ((0, 0), (0, spare))).reshape(-1)
    strength, kept = pad(time_step * coupling), pad(1.0 + time_step * growth)

    pieces = []
    for i, (start, size) in enumerate(zip(starts, CHUNKS)):
        shape = (groups, rows_of(size), 128)
        steps = size // together(size)
        early = 2 * together(size) % 8 == 0
        moved = pl.pallas_call(
            functools.partial(propagate_kernel, start),
            in_specs=[smem, smem, vmem, vmem],
            out_specs=pl.BlockSpec(memory_space=pl.ANY) if early else vmem,
            out_shape=jax.ShapeDtypeStruct(shape, jnp.float32),
            scratch_shapes=[pltpu.VMEM(shape, jnp.float32), pltpu.SemaphoreType.DMA((steps,))] if early else [],
            compiler_params=params,
            cost_estimate=pl.CostEstimate(flops=100 * size * 2048, bytes_accessed=12 * size * 2048, transcendentals=0),
            name=f"propagate_{i}",
        )(quarter, table, owns[i], halos[i])
        pieces.append(lax.all_to_all(moved, "comp", split_axis=0, concat_axis=0, tiled=True))

    total_rows = groups * group_rows
    fresh = pl.pallas_call(
        settle_kernel,
        in_specs=[smem, smem, smem] + [vmem] * len(CHUNKS),
        out_specs=vmem,
        out_shape=jax.ShapeDtypeStruct((total_rows, 128), jnp.float32),
        scratch_shapes=[pltpu.VMEM((total_rows, 128), jnp.float32)] * 5,
        compiler_params=params,
        name="settle",
    )(where, strength, kept, *pieces)

    back = lax.all_to_all(fresh.reshape(groups, group_rows, 128), "comp", split_axis=0, concat_axis=0, tiled=True)
    return pl.pallas_call(
        unpack_kernel,
        grid=(2,),
        in_specs=[vmem],
        out_specs=pl.BlockSpec((comp_dev // 2, width, height), lambda i: (i, 0, 0)),
        out_shape=jax.ShapeDtypeStruct((comp_dev, width, height), jnp.float32),
        compiler_params=params,
        name="unpack",
    )(back)


def solution(mesh):
    return jax.shard_map(
        per_device,
        mesh=mesh,
        in_specs=(P("comp", "tile", None), P("tile", None), P(), P(), P()),
        out_specs=P("comp", "tile", None),
        check_vma=False,
    )
```
